256 devices in a mesh: vseq: 32 (over x, y, z_lo), aseq: 8 (over z_hi, core).
Axes of the slice: x: 4, y: 4, z: 8 (z_hi: 4, z_lo: 2; z = z_hi * 2 + z_lo), core: 2. Of those that a mesh axis runs over, the one named last changes fastest.
Arguments:
- video_q: bfloat16 [12288, 24, 128], P(('vseq', 'aseq'))
- video_k: bfloat16 [12288, 24, 128], P(('vseq', 'aseq'))
- video_v: bfloat16 [12288, 24, 128], P(('vseq', 'aseq')), may hold values from -6 to 6
- audio_q: bfloat16 [2048, 24, 128], P(('vseq', 'aseq'))
- audio_k: bfloat16 [2048, 24, 128], P(('vseq', 'aseq'))
- audio_v: bfloat16 [2048, 24, 128], P(('vseq', 'aseq')), may hold values from -6 to 6
- video_x: bfloat16 [12288, 3072], P(('vseq', 'aseq')), may hold values from -3 to 3
- audio_x: bfloat16 [2048, 3072], P(('vseq', 'aseq')), may hold values from -3 to 3
- video_out_w: bfloat16 [3072, 3072], P('aseq'), may hold values from -0.4375 to 0.4375
- audio_out_w: bfloat16 [3072, 3072], P('aseq'), may hold values from -0.4375 to 0.4375
- video_gate_w: bfloat16 [256, 3072], replicated, may hold values from -0.375 to 0.375
- audio_gate_w: bfloat16 [256, 3072], replicated, may hold values from -0.375 to 0.375
- levels: int32 [8], replicated, may hold values from 0 to 999
- video_pos: int32 [8], replicated, may hold values from 0 to 166, as said below
- audio_pos: int32 [2048], P(('vseq', 'aseq')), may hold values from 0 to 197, as said below
Outputs:
- video_out: bfloat16 [12288, 3072], P(('vseq', 'aseq'))
- audio_out: bfloat16 [2048, 3072], P(('vseq', 'aseq'))
The draws below stay inside these ranges and needn't reach their ends.
Inputs may be any that keep to these rules, and one draw needn't show every extreme that they name: `video_pos`: the first frame lies at 0; strictly increasing, consecutive frames 16 to 32 apart; the last frame lies at 166. `audio_pos`: non-decreasing; audio token f * 256 has exactly the position video_pos[f], and tokens f * 256 to (f + 1) * 256 - 1 lie before video_pos[f + 1] where that frame exists, and within 31 of video_pos[f].
All inputs are finite; a program needn't handle non-finite values.
Results may differ from the reference program's by a relative error of at most 0.014.
Values may be sent and summed in bfloat16 or wider, within the bound.
No kernel may reach another device: no remote copies, remote signals or barrier semaphores. Data moves between devices by JAX's collectives and lax.ppermute only.
A program may use at most 128 MiB of HBM per device.

```python
import math
import jax
import jax.numpy as jnp
from jax import lax

D = 3072
HEADS = 24
HD = 128
TEMB = 256
FRAMES = 8
GRID_W = 32
LEVELS = 1000
INNER = 3072
TV = 12288
TA = 2048
FRAME_TOK = 1536
SEG = 256


def drawn_rows(key, row_total):
    return jnp.clip(1.4 * jax.random.normal(key, (row_total, HEADS, HD), jnp.float32), -5.0, 5.0)


def draw_video_q(key, part):
    values = drawn_rows(jax.random.fold_in(key, 1), TV)
    return values.astype(jnp.bfloat16)


def draw_video_k(key, part):
    values = drawn_rows(jax.random.fold_in(key, 2), TV)
    return values.astype(jnp.bfloat16)


def draw_audio_q(key, part):
    values = drawn_rows(jax.random.fold_in(key, 3), TA)
    return values.astype(jnp.bfloat16)


def draw_audio_k(key, part):
    values = drawn_rows(jax.random.fold_in(key, 4), TA)
    return values.astype(jnp.bfloat16)


def timeline(key):
    line_key = jax.random.fold_in(key, 777)
    step_index = jnp.arange(FRAMES - 1, dtype=jnp.int32)
    inner_gaps = 16 + 16 * step_index // (FRAMES - 2)
    inner_gaps = jax.random.permutation(jax.random.fold_in(line_key, 1), inner_gaps)
    gaps = jnp.concatenate([inner_gaps, jnp.full((1,), 32, jnp.int32)]).astype(jnp.int32)
    video_places = jnp.cumsum(gaps).astype(jnp.int32) - gaps
    offsets = jax.random.randint(jax.random.fold_in(line_key, 3), (FRAMES, SEG), 0, gaps[:, None], dtype=jnp.int32)
    offsets = jnp.sort(offsets.at[:, 0].set(0), axis=1)
    offsets = offsets.at[:, SEG - 1].set(gaps - 1)
    audio_places = (video_places[:, None] + offsets).reshape(TA)
    return (video_places.astype(jnp.int32), audio_places.astype(jnp.int32))


def draw_video_pos(key, part):
    video_places, audio_places = timeline(key)
    return video_places


def draw_audio_pos(key, part):
    video_places, audio_places = timeline(key)
    return audio_places


def with_ends(array, stream_key, smallest, largest):
    place = [jax.random.randint(jax.random.fold_in(stream_key, axis), (), 0, length) for axis, length in enumerate(array.shape)]
    main_axis = array.shape.index(max(array.shape))
    next_to = place[:main_axis] + [(place[main_axis] + 1) % array.shape[main_axis]] + place[main_axis + 1:]
    return array.at[tuple(place)].set(smallest).at[tuple(next_to)].set(largest)


def steps_of(rng, shape, cuts, least, top_value):
    level, own = 1.0, jax.random.fold_in(rng, 6)
    for position, shards_of in cuts:
        heights = jnp.exp(jax.random.uniform(jax.random.fold_in(own, position), (shards_of,), jnp.float32, least / len(cuts), top_value / len(cuts)))
        level = level * jnp.repeat(heights, shape[position] // shards_of).reshape([-1 if axis == position else 1 for axis in range(len(shape))])
    return level


def noise(own_key, shape, spread, reach, cuts=(), held_as=jnp.bfloat16):
    loudness = steps_of(own_key, shape, cuts, -0.22, 0.18) if cuts else 1.0
    drawn = jax.random.normal(own_key, shape, jnp.float32) * spread * loudness
    return jnp.minimum(jnp.maximum(drawn, -reach), reach).astype(held_as)


def setup_inputs(seed: int = 0) -> dict:
    arg_keys = jax.random.split(jax.random.key(seed), 16)
    return {
        "video_q": draw_video_q(jax.random.fold_in(arg_keys[15], 71), 0),
        "video_k": draw_video_k(jax.random.fold_in(arg_keys[15], 71), 0),
        "video_v": noise(arg_keys[2], (TV, HEADS, HD), 1.0, 6.0, ((0, 256),)),
        "audio_q": draw_audio_q(jax.random.fold_in(arg_keys[15], 71), 0),
        "audio_k": draw_audio_k(jax.random.fold_in(arg_keys[15], 71), 0),
        "audio_v": noise(arg_keys[5], (TA, HEADS, HD), 1.0, 6.0, ((0, 256),)),
        "video_x": noise(arg_keys[6], (TV, D), 0.5, 3.0, ((0, 256),)),
        "audio_x": noise(arg_keys[7], (TA, D), 0.5, 3.0, ((0, 256),)),
        "video_out_w": noise(arg_keys[8], (INNER, D), (INNER // 16) ** -0.5, 0.4375, ((0, 8),)),
        "audio_out_w": noise(arg_keys[9], (INNER, D), (INNER // 16) ** -0.5, 0.4375, ((0, 8),)),
        "video_gate_w": noise(arg_keys[10], (TEMB, D), TEMB ** -0.5, 0.375),
        "audio_gate_w": noise(arg_keys[11], (TEMB, D), TEMB ** -0.5, 0.375),
        "levels": with_ends(jax.random.randint(arg_keys[12], (FRAMES,), 0, LEVELS), jax.random.fold_in(arg_keys[12], 1), 0, LEVELS - 1).astype(jnp.int32),
        "video_pos": draw_video_pos(jax.random.fold_in(arg_keys[15], 71), 0),
        "audio_pos": draw_audio_pos(jax.random.fold_in(arg_keys[15], 71), 0),
    }


flow_shift = 5.0

def rotate(values, place_t, place_h, place_w):
    head_dim = values.shape[-1]
    one_sixth = head_dim // 6
    first_width = head_dim - 4 * one_sixth
    outputs = []
    sections = ((0, first_width, place_t), (first_width, 2 * one_sixth, place_h), (first_width + 2 * one_sixth, 2 * one_sixth, place_w))
    for start_col, width, places in sections:
        half_width = width // 2
        frequency = 10000.0 ** (-(jnp.arange(half_width, dtype=jnp.float32) * 2.0) / width)
        angles = places.astype(jnp.float32)[:, None] * frequency[None, :]
        cos_part = jnp.cos(angles)[:, None, :]
        sine_part = jnp.sin(angles)[:, None, :]
        low_half = values[..., start_col:start_col + half_width]
        high_half = values[..., start_col + half_width:start_col + width]
        outputs.append(low_half * cos_part - high_half * sine_part)
        outputs.append(low_half * sine_part + high_half * cos_part)
    return jnp.concatenate(outputs, axis=-1)

def frame_gates(levels, gate_w):
    level_frac = (levels.astype(jnp.float32) + 1.0) / LEVELS
    timestep = 1000.0 * flow_shift * level_frac / (1.0 + (flow_shift - 1.0) * level_frac)
    half_emb = gate_w.shape[0] // 2
    frequency = jnp.exp(-math.log(10000.0) * jnp.arange(half_emb, dtype=jnp.float32) / half_emb)
    angles = timestep[:, None] * frequency[None, :]
    embedding = jnp.concatenate([jnp.cos(angles), jnp.sin(angles)], axis=1)
    return jnp.dot(embedding, gate_w.astype(jnp.float32), precision=lax.Precision.HIGHEST, preferred_element_type=jnp.float32)

def attend(queries, keys_all, values_all):
    row_count, head_count, head_dim = queries.shape
    score_scale = 1.0 / math.sqrt(head_dim)
    block_rows = math.gcd(row_count, 512)
    query_heads = jnp.transpose(queries, (1, 0, 2))
    key_heads = jnp.transpose(keys_all, (1, 0, 2))
    value_heads = jnp.transpose(values_all, (1, 0, 2))

    def one_head(triple):
        q_head, k_head, v_head = triple
        q_blocks = q_head.reshape(row_count // block_rows, block_rows, head_dim)

        def one_block(q_block):
            scores = jnp.dot(q_block, k_head.T, preferred_element_type=jnp.float32) * score_scale
            row_max = lax.optimization_barrier(jnp.max(scores, axis=1, keepdims=True))
            weights = jnp.exp(scores - row_max)
            row_sum = lax.optimization_barrier(jnp.sum(weights, axis=1, keepdims=True))
            blended = jnp.dot(weights.astype(jnp.bfloat16), v_head, preferred_element_type=jnp.float32)
            return (blended / row_sum).astype(jnp.bfloat16)
        return lax.map(one_block, q_blocks).reshape(row_count, head_dim)
    result = lax.map(one_head, (query_heads, key_heads, value_heads))
    return jnp.transpose(result, (1, 0, 2)).reshape(row_count, head_count * head_dim)

def reference(video_q, video_k, video_v, audio_q, audio_k, audio_v, video_x, audio_x, video_out_w, audio_out_w, video_gate_w, audio_gate_w, levels, video_pos, audio_pos):
    token_index = jnp.arange(TV, dtype=jnp.int32)
    frame_of = token_index // FRAME_TOK
    within = token_index % FRAME_TOK
    place_t = video_pos[frame_of]
    place_h = within // GRID_W
    place_w = within % GRID_W
    video_query = rotate(video_q.astype(jnp.float32), place_t, place_h, place_w).astype(jnp.bfloat16)
    video_key = rotate(video_k.astype(jnp.float32), place_t, place_h, place_w).astype(jnp.bfloat16)
    audio_frame = lax.optimization_barrier(jnp.sum((video_pos[None, :] <= audio_pos[:, None]).astype(jnp.int32), axis=1)) - 1
    zero_place = jnp.zeros_like(audio_pos)
    audio_query = rotate(audio_q.astype(jnp.float32), audio_pos, zero_place, zero_place).astype(jnp.bfloat16)
    audio_key = rotate(audio_k.astype(jnp.float32), audio_pos, zero_place, zero_place).astype(jnp.bfloat16)
    keys_all = jnp.concatenate([video_key, audio_key], axis=0)
    values_all = jnp.concatenate([video_v, audio_v], axis=0)
    video_attn = attend(video_query, keys_all, values_all)
    audio_attn = attend(audio_query, keys_all, values_all)
    video_gates = frame_gates(levels, video_gate_w)
    audio_gates = frame_gates(levels, audio_gate_w)
    video_proj = jnp.dot(video_attn, video_out_w, preferred_element_type=jnp.float32)
    audio_proj = jnp.dot(audio_attn, audio_out_w, preferred_element_type=jnp.float32)
    video_out = (video_x.astype(jnp.float32) + video_gates[frame_of] * video_proj).astype(jnp.bfloat16)
    audio_out = (audio_x.astype(jnp.float32) + audio_gates[audio_frame] * audio_proj).astype(jnp.bfloat16)
    return (video_out, audio_out)
```

```python
import functools
import math

import jax
import jax.numpy as jnp
import numpy as np
from jax import lax
from jax.experimental import pallas as pl
from jax.experimental.pallas import tpu as pltpu
from jax.sharding import Mesh
from jax.sharding import PartitionSpec as P

GRID_W = 32
LEVELS = 1000
FLOW_SHIFT = 5.0
HEADS = 24
HD = 128
NX, NY, NZL, NZH, NC = 4, 4, 2, 4, 2
NZ = NZL * NZH
HPG = HEADS // NZ
TV_L = 48
TA_L = 8
T_L = TV_L + TA_L
ROWS = NZ * T_L
HALF = NZH * T_L
VHALF = NZH * TV_L
KEYS = NX * NC * ROWS
CHUNK = 512
STAT_ROWS = 64
O_ROWS = HPG * ROWS + STAT_ROWS
AXES = ("x", "y", "zl", "zh", "c")
VMEM = pl.BlockSpec(memory_space=pltpu.VMEM)
ANY = pl.BlockSpec(memory_space=pl.ANY)
NT = (((1,), (1,)), ((), ()))
TN = (((0,), (0,)), ((), ()))


def rope_lanes():
    sixth = HD // 6
    first = HD - 4 * sixth
    partner = np.zeros(HD, np.int32)
    sign = np.zeros(HD, np.float32)
    index = np.zeros(HD, np.float32)
    width_of = np.zeros(HD, np.float32)
    section = np.zeros(HD, np.int32)
    for number, (start, width) in enumerate(
        ((0, first), (first, 2 * sixth), (first + 2 * sixth, 2 * sixth))
    ):
        half = width // 2
        for k in range(half):
            low, high = start + k, start + half + k
            partner[low], partner[high] = high, low
            sign[low], sign[high] = -1.0, 1.0
            index[low] = index[high] = k
            width_of[low] = width_of[high] = width
            section[low] = section[high] = number
    return partner, sign, index, width_of, section


PARTNER, SIGN, INDEX, WIDTH_OF, SECTION = rope_lanes()


def group_of(z):
    return (z % NZH) * NZL + z // NZH


def prep_kernel(vq, vk, vv, aq, ak, av, swap, cos, sin, out):
    scale = math.log2(math.e) / math.sqrt(HD)
    cos_v, sin_v = cos[0:TV_L, :], sin[0:TV_L, :]
    cos_a, sin_a = cos[TV_L:T_L, :], sin[TV_L:T_L, :]
    tables = (
        (cos_v * scale, sin_v * scale, cos_a * scale, sin_a * scale),
        (cos_v, sin_v, cos_a, sin_a),
    )
    perm = swap[...]

    def turn(u, cos_part, sin_part):
        other = jnp.dot(u, perm, preferred_element_type=jnp.float32)
        return (u.astype(jnp.float32) * cos_part + other * sin_part).astype(jnp.bfloat16)

    for z in range(NZ):
        for h in range(HPG):
            lanes = slice((group_of(z) * HPG + h) * HD, (group_of(z) * HPG + h + 1) * HD)
            for t, (video, audio) in enumerate(((vq, aq), (vk, ak))):
                cv, sv, ca, sa = tables[t]
                out[z, t, h, 0:TV_L, :] = turn(video[:, lanes], cv, sv)
                out[z, t, h, TV_L:T_L, :] = turn(audio[:, lanes], ca, sa)
            out[z, 2, h, 0:TV_L, :] = vv[:, lanes]
            out[z, 2, h, TV_L:T_L, :] = av[:, lanes]


def arrange_kernel(got, q_out, kv_out):
    for z in range(NZ):
        zl, zh = z // NZH, z % NZH
        v_at = zl * HALF + zh * TV_L
        a_at = zl * HALF + VHALF + zh * TA_L
        for h in range(HPG):
            q_out[h, v_at : v_at + TV_L, :] = got[z, 0, h, 0:TV_L, :]
            q_out[h, a_at : a_at + TA_L, :] = got[z, 0, h, TV_L:T_L, :]
            for t in range(2):
                kv_out[t, h, v_at : v_at + TV_L, :] = got[z, 1 + t, h, 0:TV_L, :]
                kv_out[t, h, a_at : a_at + TA_L, :] = got[z, 1 + t, h, TV_L:T_L, :]


def attn_kernel(*refs):
    qs = refs[0:NY]
    kvs = refs[NY : NY + NX * NC]
    outs = refs[NY + NX * NC : NY + NX * NC + NY]
    qc, kc, vc, sc, mc, oc, lc, sems = refs[NY + NX * NC + NY :]
    n_kv = NX * NC
    copies = []
    for h in range(HPG):
        for a in range(n_kv):
            rows = pl.ds(a * ROWS, ROWS)
            copies.append(
                pltpu.make_async_copy(
                    kvs[a].at[0, h], kc.at[h, rows, :], sems.at[h * 2 * n_kv + 2 * a]
                )
            )
            copies.append(
                pltpu.make_async_copy(
                    kvs[a].at[1, h],
                    vc.at[h, rows, pl.ds(0, HD)],
                    sems.at[h * 2 * n_kv + 2 * a + 1],
                )
            )
    for copy in copies:
        copy.start()
    for h in range(HPG):
        vc[h, :, HD : 2 * HD] = jnp.ones((KEYS, HD), jnp.bfloat16)
        for s in range(NY):
            qc[h * NY + s] = qs[s][h]
    for copy in copies:
        copy.wait()
    n_chunks = KEYS // CHUNK

    def scores(tile, head, j, slot, top):
        s = lax.dot_general(
            qc[tile], kc[head, j * CHUNK : (j + 1) * CHUNK, :], NT,
            preferred_element_type=jnp.float32,
        )
        sc[slot, :, j * CHUNK : (j + 1) * CHUNK] = s
        part = s[:, 0:HD]
        for g in range(1, CHUNK // HD):
            part = jnp.maximum(part, s[:, g * HD : (g + 1) * HD])
        return part if top is None else jnp.maximum(top, part)

    def settle(top, slot):
        mc[slot] = jnp.broadcast_to(jnp.max(top, axis=1, keepdims=True), (ROWS, HD))

    def blend(head, j, slot, peak, total):
        s = sc[slot, :, j * CHUNK : (j + 1) * CHUNK]
        weights = jnp.concatenate(
            [
                jnp.exp2(s[:, g * HD : (g + 1) * HD] - peak).astype(jnp.bfloat16)
                for g in range(CHUNK // HD)
            ],
            axis=1,
        )
        new = jnp.dot(
            weights, vc[head, j * CHUNK : (j + 1) * CHUNK, :],
            preferred_element_type=jnp.float32,
        )
        return new if total is None else total + new

    def store(tile, peak, total):
        mass = total[:, HD : 2 * HD]
        oc[tile] = (total[:, 0:HD] / mass).astype(jnp.bfloat16)
        lc[tile] = peak + jnp.log2(mass)

    top = None
    for j in range(n_chunks):
        top = scores(0, 0, j, 0, top)
    settle(top, 0)

    def body(tile, carry):
        slot = lax.rem(tile, 2)
        head = tile // NY
        following = tile + 1
        next_head = following // NY
        peak = mc[slot]
        top, total = None, None
        for j in range(n_chunks):
            top = scores(following, next_head, j, 1 - slot, top)
            total = blend(head, j, slot, peak, total)
        settle(top, 1 - slot)
        store(tile, peak, total)
        return carry

    last = HPG * NY - 1
    lax.fori_loop(0, last, body, 0)
    peak = mc[last % 2]
    total = None
    for j in range(n_chunks):
        total = blend(HPG - 1, j, last % 2, peak, total)
    store(last, peak, total)

    lane = lax.broadcasted_iota(jnp.int32, (ROWS, HD), 1)
    eye = (
        lax.broadcasted_iota(jnp.int32, (16, HD), 0)
        == lax.broadcasted_iota(jnp.int32, (16, HD), 1)
    ).astype(jnp.bfloat16)
    for s in range(NY):
        stat = jnp.zeros((ROWS, HD), jnp.float32)
        for h in range(HPG):
            outs[s][h * ROWS : (h + 1) * ROWS, :] = oc[h * NY + s]
            level = lc[h * NY + s]
            for piece in range(3):
                short = level.astype(jnp.bfloat16).astype(jnp.float32)
                stat = jnp.where(lane == 3 * h + piece, short, stat)
                level = level - short
        turned = lax.dot_general(
            eye, stat.astype(jnp.bfloat16), NT, preferred_element_type=jnp.float32
        ).astype(jnp.bfloat16)
        turned = jnp.concatenate([turned, jnp.zeros((16, 4 * HD - ROWS), jnp.bfloat16)], axis=1)
        for g in range(4):
            at = HPG * ROWS + 16 * g
            outs[s][at : at + 16, :] = turned[:, g * HD : (g + 1) * HD]


def merge_kernel(zl_ref, o0, o1, o2, o3, keep, send, lm):
    eye = (
        lax.broadcasted_iota(jnp.int32, (16, HD), 0)
        == lax.broadcasted_iota(jnp.int32, (16, HD), 1)
    ).astype(jnp.bfloat16)
    parts = (o0, o1, o2, o3)
    for s, part in enumerate(parts):
        for g in range(4):
            at = HPG * ROWS + 16 * g
            lm[s, g * HD : (g + 1) * HD, :] = lax.dot_general(
                part[at : at + 16, :], eye, TN, preferred_element_type=jnp.float32
            )
    zl = zl_ref[0]
    for target, half in ((keep, zl), (send, 1 - zl)):
        off = pl.multiple_of(half * HALF, 32)
        stats = [lm[s, pl.ds(off, HALF), :] for s in range(NY)]
        for h in range(HPG):
            levels = [
                st[:, 3 * h : 3 * h + 1] + st[:, 3 * h + 1 : 3 * h + 2] + st[:, 3 * h + 2 : 3 * h + 3]
                for st in stats
            ]
            peak = functools.reduce(jnp.maximum, levels)
            shares = [jnp.exp2(level - peak) for level in levels]
            mass = functools.reduce(jnp.add, shares)
            total = None
            for s, part in enumerate(parts):
                rows = part[pl.ds(pl.multiple_of(h * ROWS + off, 32), HALF), :].astype(jnp.float32)
                term = rows * (shares[s] / mass)
                total = term if total is None else total + term
            target[:, h * HD : (h + 1) * HD] = total.astype(jnp.bfloat16)


def project_kernel(a_mine, a_other, wv_mine, wv_other, wa_mine, wa_other, out):
    def product(rows, mine, other):
        return (
            jnp.dot(a_mine[rows, :], mine[...], preferred_element_type=jnp.float32)
            + jnp.dot(a_other[rows, :], other[...], preferred_element_type=jnp.float32)
        ).astype(jnp.bfloat16)

    video = product(slice(0, VHALF), wv_mine, wv_other)
    audio = product(slice(VHALF, HALF), wa_mine, wa_other)
    for zh in range(NZH):
        out[zh, 0:TV_L, :] = video[zh * TV_L : (zh + 1) * TV_L, :]
        out[zh, TV_L:T_L, :] = audio[zh * TA_L : (zh + 1) * TA_L, :]


def params(mib):
    return pltpu.CompilerParams(vmem_limit_bytes=mib << 20)


def shift(array, axis, step, size):
    return lax.ppermute(array, axis, [(i, (i + step) % size) for i in range(size)])


def frame_gate(levels, frame, gate_w):
    level = lax.dynamic_slice(levels, (frame,), (1,)).astype(jnp.float32)
    level_frac = (level + 1.0) / LEVELS
    timestep = 1000.0 * FLOW_SHIFT * level_frac / (1.0 + (FLOW_SHIFT - 1.0) * level_frac)
    half_emb = gate_w.shape[0] // 2
    frequency = jnp.exp(-math.log(10000.0) * jnp.arange(half_emb, dtype=jnp.float32) / half_emb)
    angles = timestep[:, None] * frequency[None, :]
    embedding = jnp.concatenate([jnp.cos(angles), jnp.sin(angles)], axis=1)
    return jnp.dot(
        embedding,
        gate_w.astype(jnp.float32),
        precision=lax.Precision.HIGHEST,
        preferred_element_type=jnp.float32,
    )


def local(
    video_q, video_k, video_v, audio_q, audio_k, audio_v, video_x, audio_x,
    video_out_w, audio_out_w, video_gate_w, audio_gate_w, levels, video_pos, audio_pos,
):
    rank = lax.axis_index(AXES)
    width = HEADS * HD
    per_frame = NX * NY * NZ * NC // video_pos.shape[0]
    frame = rank // per_frame

    within = lax.rem(rank, per_frame) * TV_L + jnp.arange(TV_L, dtype=jnp.int32)
    place_t = jnp.concatenate(
        [jnp.broadcast_to(lax.dynamic_slice(video_pos, (frame,), (1,)), (TV_L,)), audio_pos]
    )
    zeros = jnp.zeros((TA_L,), jnp.int32)
    place_h = jnp.concatenate([within // GRID_W, zeros])
    place_w = jnp.concatenate([within % GRID_W, zeros])
    frequency = 10000.0 ** (-(jnp.asarray(INDEX) * 2.0) / jnp.asarray(WIDTH_OF))
    section = jnp.asarray(SECTION)[None, :]
    place = jnp.where(
        section == 0,
        place_t[:, None],
        jnp.where(section == 1, place_h[:, None], place_w[:, None]),
    ).astype(jnp.float32)
    angles = place * frequency[None, :]
    cos = jnp.cos(angles)
    sin = jnp.sin(angles) * jnp.asarray(SIGN)[None, :]
    swap = (jnp.arange(HD)[:, None] == jnp.asarray(PARTNER)[None, :]).astype(jnp.bfloat16)

    packed = pl.pallas_call(
        prep_kernel,
        out_shape=jax.ShapeDtypeStruct((NZ, 3, HPG, T_L, HD), jnp.bfloat16),
        in_specs=[VMEM] * 9,
        out_specs=VMEM,
        compiler_params=params(32),
    )(
        video_q.reshape(TV_L, width), video_k.reshape(TV_L, width), video_v.reshape(TV_L, width),
        audio_q.reshape(TA_L, width), audio_k.reshape(TA_L, width), audio_v.reshape(TA_L, width),
        swap, cos, sin,
    )
    got = lax.all_to_all(packed, ("zl", "zh"), split_axis=0, concat_axis=0, tiled=True)
    q_mine, kv_mine = pl.pallas_call(
        arrange_kernel,
        out_shape=(
            jax.ShapeDtypeStruct((HPG, ROWS, HD), jnp.bfloat16),
            jax.ShapeDtypeStruct((2, HPG, ROWS, HD), jnp.bfloat16),
        ),
        in_specs=[VMEM],
        out_specs=(VMEM, VMEM),
        compiler_params=params(32),
    )(got)

    kv_x = [kv_mine] + [shift(kv_mine, "x", s, NX) for s in (1, 3, 2)]
    kv_all = kv_x + [shift(kv, "c", 1, NC) for kv in kv_x]
    steps = (0, 1, 3, 2)
    q_all = [q_mine] + [shift(q_mine, "y", s, NY) for s in steps[1:]]
    wv_other = shift(video_out_w, "c", 1, NC)
    wa_other = shift(audio_out_w, "c", 1, NC)

    o_shape = jax.ShapeDtypeStruct((O_ROWS, HD), jnp.bfloat16)
    partial = pl.pallas_call(
        attn_kernel,
        out_shape=(o_shape,) * NY,
        in_specs=[VMEM] * NY + [ANY] * (NX * NC),
        out_specs=(VMEM,) * NY,
        scratch_shapes=[
            pltpu.VMEM((HPG * NY, ROWS, HD), jnp.bfloat16),
            pltpu.VMEM((HPG, KEYS, HD), jnp.bfloat16),
            pltpu.VMEM((HPG, KEYS, 2 * HD), jnp.bfloat16),
            pltpu.VMEM((2, ROWS, KEYS), jnp.float32),
            pltpu.VMEM((2, ROWS, HD), jnp.float32),
            pltpu.VMEM((HPG * NY, ROWS, HD), jnp.bfloat16),
            pltpu.VMEM((HPG * NY, ROWS, HD), jnp.float32),
            pltpu.SemaphoreType.DMA((HPG * 2 * NX * NC,)),
        ],
        compiler_params=params(52),
        cost_estimate=pl.CostEstimate(
            flops=4 * HPG * NY * ROWS * KEYS * HD,
            bytes_accessed=10 << 20,
            transcendentals=HPG * NY * ROWS * KEYS,
        ),
    )(*q_all, *kv_all)
    back = [partial[0]] + [
        shift(partial[i], "y", NY - steps[i], NY) for i in range(1, NY)
    ]
    zl = lax.axis_index("zl")
    c = lax.axis_index("c")
    a_shape = jax.ShapeDtypeStruct((HALF, HPG * HD), jnp.bfloat16)
    keep, send = pl.pallas_call(
        merge_kernel,
        out_shape=(a_shape, a_shape),
        in_specs=[pl.BlockSpec(memory_space=pltpu.SMEM)] + [VMEM] * NY,
        out_specs=(VMEM, VMEM),
        scratch_shapes=[pltpu.VMEM((NY, 4 * HD, HD), jnp.float32)],
        compiler_params=params(32),
    )(jnp.full((1,), zl, jnp.int32), *back)
    came = shift(send, "zl", 1, NZL)
    same = zl == c
    a_mine = jnp.where(same, keep, came)
    a_other = jnp.where(same, came, keep)

    cols = 768
    a_spec = pl.BlockSpec((HALF, HPG * HD), lambda i: (0, 0))
    w_spec = pl.BlockSpec((HPG * HD, cols), lambda i: (0, i))
    shares = pl.pallas_call(
        project_kernel,
        grid=(width // cols,),
        out_shape=jax.ShapeDtypeStruct((NZH, T_L, width), jnp.bfloat16),
        in_specs=[a_spec, a_spec, w_spec, w_spec, w_spec, w_spec],
        out_specs=pl.BlockSpec((NZH, T_L, cols), lambda i: (0, 0, i)),
        compiler_params=params(32),
    )(a_mine, a_other, video_out_w, wv_other, audio_out_w, wa_other)
    summed = lax.all_to_all(shares, "zh", split_axis=0, concat_axis=0, tiled=True)
    proj = jnp.sum(summed.astype(jnp.float32), axis=0)
    video_gate = frame_gate(levels, frame, video_gate_w)
    audio_gate = frame_gate(levels, frame, audio_gate_w)
    video_out = (video_x.astype(jnp.float32) + video_gate * proj[:TV_L]).astype(jnp.bfloat16)
    audio_out = (audio_x.astype(jnp.float32) + audio_gate * proj[TV_L:]).astype(jnp.bfloat16)
    return (video_out, audio_out)


def solution(mesh):
    fine = Mesh(mesh.devices.reshape(NX, NY, NZL, NZH, NC), AXES)
    tokens3 = P(AXES, None, None)
    tokens2 = P(AXES, None)
    weights = P(("zh", "c"), None)
    return jax.shard_map(
        local,
        mesh=fine,
        in_specs=(
            tokens3, tokens3, tokens3, tokens3, tokens3, tokens3,
            tokens2, tokens2, weights, weights, P(), P(), P(), P(), P(AXES),
        ),
        out_specs=(tokens2, tokens2),
        check_vma=False,
    )
```

```python
import functools
import math

import jax
import jax.numpy as jnp
import numpy as np
from jax import lax
from jax.experimental import pallas as pl
from jax.experimental.pallas import tpu as pltpu
from jax.sharding import Mesh
from jax.sharding import PartitionSpec as P

GRID_W = 32
GRID_SHIFT = 5
LEVELS = 1000
FLOW_SHIFT = 5.0
HEADS = 24
HD = 128
NX, NY, NZL, NZH, NC = 4, 4, 2, 4, 2
NZ = NZL * NZH
HPG = HEADS // NZ
TV_L = 48
TA_L = 8
T_L = TV_L + TA_L
ROWS = NZ * T_L
HALF = NZH * T_L
VHALF = NZH * TV_L
CHUNK = 512
STAT = 16
AXES = ("x", "y", "zl", "zh", "c")
VMEM = pl.BlockSpec(memory_space=pltpu.VMEM)
SMEM = pl.BlockSpec(memory_space=pltpu.SMEM)
ANY = pl.BlockSpec(memory_space=pl.ANY)
NT = (((1,), (1,)), ((), ()))
TN = (((0,), (0,)), ((), ()))


def rope_lanes():
    sixth = HD // 6
    first = HD - 4 * sixth
    partner = np.zeros(HD, np.int32)
    sign = np.zeros(HD, np.float32)
    index = np.zeros(HD, np.float32)
    width_of = np.zeros(HD, np.float32)
    section = np.zeros(HD, np.int32)
    for number, (start, width) in enumerate(
        ((0, first), (first, 2 * sixth), (first + 2 * sixth, 2 * sixth))
    ):
        half = width // 2
        for k in range(half):
            low, high = start + k, start + half + k
            partner[low], partner[high] = high, low
            sign[low], sign[high] = -1.0, 1.0
            index[low] = index[high] = k
            width_of[low] = width_of[high] = width
            section[low] = section[high] = number
    return partner, sign, index, width_of, section


PARTNER, SIGN, INDEX, WIDTH_OF, SECTION = rope_lanes()


def group_of(z):
    return (z % NZH) * NZL + z // NZH


def prep_kernel(vpos, apos, vq, vk, vv, aq, ak, av, swap, tables, out):
    scale = math.log2(math.e) / math.sqrt(HD)
    rank = jnp.int32(0)
    for name, size in zip(AXES, (NX, NY, NZL, NZH, NC)):
        rank = rank * size + lax.axis_index(name)
    per_frame = NX * NY * NZ * NC // vpos.shape[0]
    frame = lax.div(rank, jnp.int32(per_frame))
    start = lax.rem(rank, jnp.int32(per_frame)) * TV_L
    row_v = lax.broadcasted_iota(jnp.int32, (TV_L, HD), 0)
    row_a = lax.broadcasted_iota(jnp.int32, (TA_L, HD), 0)
    within = start + row_v
    high = within >> GRID_SHIFT
    wide = within & (GRID_W - 1)
    section_v = jnp.broadcast_to(tables[2:3, :], (TV_L, HD))
    place_v = jnp.where(
        section_v == 0.0,
        vpos[frame].astype(jnp.float32),
        jnp.where(section_v == 1.0, high.astype(jnp.float32), wide.astype(jnp.float32)),
    )
    place_a = jnp.zeros((TA_L, HD), jnp.int32)
    for i in range(TA_L):
        place_a = jnp.where(row_a == i, apos[i], place_a)
    section_a = jnp.broadcast_to(tables[2:3, :], (TA_L, HD))
    place_a = jnp.where(section_a == 0.0, place_a.astype(jnp.float32), 0.0)
    perm = swap[...]

    def turn(ref, place, gain):
        n, heads, hd = ref.shape
        angles = place * tables[0:1, :]
        cos = jnp.cos(angles) * gain
        sin = jnp.sin(angles) * tables[1:2, :] * gain
        u = jnp.swapaxes(ref[...], 0, 1)
        other = jnp.dot(
            u.reshape(heads * n, hd), perm, preferred_element_type=jnp.float32
        ).reshape(heads, n, hd)
        return (u.astype(jnp.float32) * cos[None] + other * sin[None]).astype(jnp.bfloat16)

    for t, (video, audio, gain) in enumerate(((vq, aq, scale), (vk, ak, 1.0), (vv, av, None))):
        if gain is None:
            video, audio = jnp.swapaxes(video[...], 0, 1), jnp.swapaxes(audio[...], 0, 1)
        else:
            video, audio = turn(video, place_v, gain), turn(audio, place_a, gain)
        for z in range(NZ):
            for h in range(HPG):
                out[z, t, h, 0:TV_L, :] = video[group_of(z) * HPG + h]
                out[z, t, h, TV_L:T_L, :] = audio[group_of(z) * HPG + h]


def arrange_kernel(got, q_out, kv_out):
    for z in range(NZ):
        zl, zh = z // NZH, z % NZH
        v_at = zl * HALF + zh * TV_L
        a_at = zl * HALF + VHALF + zh * TA_L
        for h in range(HPG):
            q_out[h, v_at : v_at + TV_L, :] = got[z, 0, h, 0:TV_L, :]
            q_out[h, a_at : a_at + TA_L, :] = got[z, 0, h, TV_L:T_L, :]
            for t in range(2):
                kv_out[t, h, v_at : v_at + TV_L, :] = got[z, 1 + t, h, 0:TV_L, :]
                kv_out[t, h, a_at : a_at + TA_L, :] = got[z, 1 + t, h, TV_L:T_L, :]


def eye_tile():
    return (
        lax.broadcasted_iota(jnp.int32, (STAT, HD), 0)
        == lax.broadcasted_iota(jnp.int32, (STAT, HD), 1)
    ).astype(jnp.bfloat16)


def stat_tile(level):
    lane = lax.broadcasted_iota(jnp.int32, (ROWS, HD), 1)
    row = lax.broadcasted_iota(jnp.int32, (ROWS, HD), 0)
    stat = jnp.zeros((ROWS, HD), jnp.float32)
    for piece in range(3):
        short = level.astype(jnp.bfloat16).astype(jnp.float32)
        stat = jnp.where(lane == 3 * (row >> 7) + piece, short, stat)
        level = level - short
    stat = stat.astype(jnp.bfloat16)
    tile = None
    for at in range(0, ROWS, HD):
        size = min(HD, ROWS - at)
        part = lax.dot_general(
            eye_tile(), stat[at : at + size, :], NT, preferred_element_type=jnp.float32
        )
        if size < HD:
            part = jnp.concatenate([part, jnp.zeros((STAT, HD - size), jnp.float32)], axis=1)
        tile = part if tile is None else tile + part
    return tile.astype(jnp.bfloat16)


def stat_level(tile):
    flat = lax.dot_general(tile, eye_tile(), TN, preferred_element_type=jnp.float32)
    pieces = []
    for g in range(-(-ROWS // HD)):
        size = min(HD, ROWS - g * HD)
        pieces.append(
            flat[0:size, 3 * g : 3 * g + 1]
            + flat[0:size, 3 * g + 1 : 3 * g + 2]
            + flat[0:size, 3 * g + 2 : 3 * g + 3]
        )
    return jnp.broadcast_to(jnp.concatenate(pieces, axis=0), (ROWS, HD))


def attn_kernel(n_q, n_pair, n_split, with_prev, final, *refs):
    refs = list(refs)

    def take(count):
        taken, refs[:count] = refs[:count], []
        return taken

    qs, pairs, splits = take(n_q), take(n_pair), take(2 * n_split)
    prev = take(2) if with_prev else None
    outs = take(n_q if final else 2)
    qc, kc, vc, oc, lc, sems = refs
    n_kv = n_pair + n_split
    rows, keys = n_q * ROWS, n_kv * ROWS
    copies = []
    for h in range(HPG):
        for a in range(n_kv):
            if a < n_pair:
                k_from, v_from = pairs[a].at[0, h], pairs[a].at[1, h]
            else:
                k_from, v_from = (ref.at[h] for ref in splits[2 * (a - n_pair) :][:2])
            place = pl.ds(a * ROWS, ROWS)
            at = 2 * (h * n_kv + a)
            copies.append(pltpu.make_async_copy(k_from, kc.at[h, place, :], sems.at[at]))
            copies.append(
                pltpu.make_async_copy(v_from, vc.at[h, place, pl.ds(0, HD)], sems.at[at + 1])
            )
    for copy in copies:
        copy.start()
    for h in range(HPG):
        vc[h, :, HD : 2 * HD] = jnp.ones((keys, HD), jnp.bfloat16)
        for s in range(n_q):
            qc[h, s * ROWS : (s + 1) * ROWS, :] = qs[s][h]
    for copy in copies:
        copy.wait()
    cuts = [(at, min(CHUNK, keys - at)) for at in range(0, keys, CHUNK)]

    def body(head, carry):
        queries = qc[head]

        def scores(cut):
            at, size = cut
            return lax.dot_general(
                queries, kc[head, at : at + size, :], NT, preferred_element_type=jnp.float32
            )

        s = scores(cuts[0])
        peak = total = None
        for number, (at, size) in enumerate(cuts):
            coming = scores(cuts[number + 1]) if number + 1 < len(cuts) else None
            slabs = [s[:, g : g + HD] for g in range(0, size, HD)]
            top = jnp.max(functools.reduce(jnp.maximum, slabs), axis=1, keepdims=True)
            top = jnp.broadcast_to(top, (rows, HD))
            if peak is not None:
                top = jnp.maximum(peak, top)
            weights = jnp.concatenate(
                [jnp.exp2(slab - top).astype(jnp.bfloat16) for slab in slabs], axis=1
            )
            new = jnp.dot(
                weights, vc[head, at : at + size, :], preferred_element_type=jnp.float32
            )
            if total is None:
                total = new
            else:
                factor = jnp.exp2(peak - top)
                total = total * jnp.concatenate([factor, factor], axis=1) + new
            peak, s = top, coming
        mass = total[:, HD : 2 * HD]
        oc[head] = total[:, 0:HD] / mass
        lc[head] = peak + jnp.log2(mass)
        return carry

    lax.fori_loop(0, HPG, body, 0)
    for h in range(HPG):
        for s in range(n_q):
            span = slice(s * ROWS, (s + 1) * ROWS)
            value, level = oc[h, span, :], lc[h, span, :]
            if with_prev:
                at = (h * n_q + s) * STAT
                before = stat_level(prev[1][at : at + STAT, :])
                top = jnp.maximum(level, before)
                here, there = jnp.exp2(level - top), jnp.exp2(before - top)
                both = here + there
                value = (value * here + prev[0][h, span, :] * there) / both
                level = top + jnp.log2(both)
            if final:
                at = h * (ROWS + STAT)
                outs[s][at : at + ROWS, :] = value.astype(jnp.bfloat16)
                outs[s][at + ROWS : at + ROWS + STAT, :] = stat_tile(level)
            else:
                outs[0][h, span, :] = value
                outs[1][(h * n_q + s) * STAT : (h * n_q + s + 1) * STAT, :] = stat_tile(level)


def attention(queries, pairs, splits, prev, final):
    n_q, n_pair, n_split = len(queries), len(pairs), len(splits) // 2
    rows, keys = n_q * ROWS, (n_pair + n_split) * ROWS
    if final:
        shapes = (jax.ShapeDtypeStruct((HPG * (ROWS + STAT), HD), jnp.bfloat16),) * n_q
    else:
        shapes = (
            jax.ShapeDtypeStruct((HPG, rows, HD), jnp.float32),
            jax.ShapeDtypeStruct((HPG * n_q * STAT, HD), jnp.bfloat16),
        )
    prev = () if prev is None else tuple(prev)
    return pl.pallas_call(
        functools.partial(attn_kernel, n_q, n_pair, n_split, bool(prev), final),
        out_shape=shapes,
        in_specs=[VMEM] * n_q + [ANY] * (n_pair + 2 * n_split) + [VMEM] * len(prev),
        out_specs=(VMEM,) * len(shapes),
        scratch_shapes=[
            pltpu.VMEM((HPG, rows, HD), jnp.bfloat16),
            pltpu.VMEM((HPG, keys, HD), jnp.bfloat16),
            pltpu.VMEM((HPG, keys, 2 * HD), jnp.bfloat16),
            pltpu.VMEM((HPG, rows, HD), jnp.float32),
            pltpu.VMEM((HPG, rows, HD), jnp.float32),
            pltpu.SemaphoreType.DMA((2 * HPG * (n_pair + n_split),)),
        ],
        compiler_params=params(52),
        cost_estimate=pl.CostEstimate(
            flops=16 * HPG * rows * keys * HD,
            bytes_accessed=8 << 20,
            transcendentals=HPG * rows * keys,
        ),
    )(*queries, *pairs, *splits, *prev)


def merge_kernel(zl_ref, o0, o1, o2, o3, keep, send, merged):
    parts = (o0, o1, o2, o3)
    for h in range(HPG):
        at = h * (ROWS + STAT)
        levels = [stat_level(part[at + ROWS : at + ROWS + STAT, :]) for part in parts]
        peak = functools.reduce(jnp.maximum, levels)
        shares = [jnp.exp2(level - peak) for level in levels]
        mass = functools.reduce(jnp.add, shares)
        total = functools.reduce(
            jnp.add,
            [part[at : at + ROWS, :].astype(jnp.float32) * w for part, w in zip(parts, shares)],
        )
        merged[:, h * HD : (h + 1) * HD] = (total / mass).astype(jnp.bfloat16)
    zl = zl_ref[0]
    keep[...] = merged[pl.ds(pl.multiple_of(zl * HALF, 32), HALF), :]
    send[...] = merged[pl.ds(pl.multiple_of((1 - zl) * HALF, 32), HALF), :]


def project_kernel(a_mine, a_other, wv_mine, wv_other, wa_mine, wa_other, out):
    def product(rows, mine, other):
        return (
            jnp.dot(a_mine[rows, :], mine[...], preferred_element_type=jnp.float32)
            + jnp.dot(a_other[rows, :], other[...], preferred_element_type=jnp.float32)
        ).astype(jnp.bfloat16)

    video = product(slice(0, VHALF), wv_mine, wv_other)
    audio = product(slice(VHALF, HALF), wa_mine, wa_other)
    for zh in range(NZH):
        out[zh, 0:TV_L, :] = video[zh * TV_L : (zh + 1) * TV_L, :]
        out[zh, TV_L:T_L, :] = audio[zh * TA_L : (zh + 1) * TA_L, :]


def params(mib):
    return pltpu.CompilerParams(vmem_limit_bytes=mib << 20)


def shift(array, axis, step, size):
    return lax.ppermute(array, axis, [(i, (i + step) % size) for i in range(size)])


def frame_gate(levels, frame, gate_w):
    level = lax.dynamic_slice(levels, (frame,), (1,)).astype(jnp.float32)
    level_frac = (level + 1.0) / LEVELS
    timestep = 1000.0 * FLOW_SHIFT * level_frac / (1.0 + (FLOW_SHIFT - 1.0) * level_frac)
    half_emb = gate_w.shape[0] // 2
    frequency = jnp.exp(-math.log(10000.0) * jnp.arange(half_emb, dtype=jnp.float32) / half_emb)
    angles = timestep[:, None] * frequency[None, :]
    embedding = jnp.concatenate([jnp.cos(angles), jnp.sin(angles)], axis=1)
    return jnp.dot(
        embedding,
        gate_w.astype(jnp.float32),
        precision=lax.Precision.HIGHEST,
        preferred_element_type=jnp.float32,
    )


def local(
    video_q, video_k, video_v, audio_q, audio_k, audio_v, video_x, audio_x,
    video_out_w, audio_out_w, video_gate_w, audio_gate_w, levels, video_pos, audio_pos,
):
    width = HEADS * HD
    rank = lax.axis_index(AXES)
    frame = rank // (NX * NY * NZ * NC // video_pos.shape[0])
    frequency = 10000.0 ** (-(INDEX * np.float32(2.0)) / WIDTH_OF)
    tables = jnp.asarray(
        np.concatenate(
            [
                np.stack([frequency, SIGN, SECTION]).astype(np.float32),
                np.zeros((5, HD), np.float32),
            ]
        )
    )
    swap = jnp.asarray(np.arange(HD)[:, None] == PARTNER[None, :], jnp.bfloat16)
    packed = pl.pallas_call(
        prep_kernel,
        out_shape=jax.ShapeDtypeStruct((NZ, 3, HPG, T_L, HD), jnp.bfloat16),
        in_specs=[SMEM] * 2 + [VMEM] * 8,
        out_specs=VMEM,
        compiler_params=params(32),
    )(
        video_pos, audio_pos, video_q, video_k, video_v, audio_q, audio_k, audio_v, swap, tables
    )
    got = lax.all_to_all(packed, ("zl", "zh"), split_axis=0, concat_axis=0, tiled=True)
    q_mine, kv_mine = pl.pallas_call(
        arrange_kernel,
        out_shape=(
            jax.ShapeDtypeStruct((HPG, ROWS, HD), jnp.bfloat16),
            jax.ShapeDtypeStruct((2, HPG, ROWS, HD), jnp.bfloat16),
        ),
        in_specs=[VMEM],
        out_specs=(VMEM, VMEM),
        compiler_params=params(32),
    )(got)

    kv_left = shift(kv_mine, "x", 1, NX)
    kv_right = shift(kv_mine, "x", NX - 1, NX)
    steps = (1, NY - 1, 2)
    q_far = [shift(q_mine, "y", step, NY) for step in steps]
    pairs = [kv_mine, kv_left, kv_right]
    k_far = shift(kv_left[0], "x", 1, NX)
    v_far = shift(kv_right[1], "x", NX - 1, NX)
    pairs = pairs + [shift(kv, "c", 1, NC) for kv in pairs]
    wv_other = shift(video_out_w, "c", 1, NC)
    wa_other = shift(audio_out_w, "c", 1, NC)

    first = attention(q_far, pairs, [], None, False)
    k_far, v_far, *first = lax.optimization_barrier((k_far, v_far, *first))
    splits = [k_far, v_far, shift(k_far, "c", 1, NC), shift(v_far, "c", 1, NC)]
    partial = attention(q_far, [], splits, first, True)
    back = [shift(part, "y", NY - step, NY) for part, step in zip(partial, steps)]
    own = attention([q_mine], pairs, splits, None, True)
    back = list(own) + back
    zl = lax.axis_index("zl")
    c = lax.axis_index("c")
    a_shape = jax.ShapeDtypeStruct((HALF, HPG * HD), jnp.bfloat16)
    keep, send = pl.pallas_call(
        merge_kernel,
        out_shape=(a_shape, a_shape),
        in_specs=[SMEM] + [VMEM] * NY,
        out_specs=(VMEM, VMEM),
        scratch_shapes=[pltpu.VMEM((ROWS, HPG * HD), jnp.bfloat16)],
        compiler_params=params(32),
    )(jnp.full((1,), zl, jnp.int32), *back)
    came = shift(send, "zl", 1, NZL)
    same = zl == c
    a_mine = jnp.where(same, keep, came)
    a_other = jnp.where(same, came, keep)

    cols = 768
    a_spec = pl.BlockSpec((HALF, HPG * HD), lambda i: (0, 0))
    w_spec = pl.BlockSpec((HPG * HD, cols), lambda i: (0, i))
    shares = pl.pallas_call(
        project_kernel,
        grid=(width // cols,),
        out_shape=jax.ShapeDtypeStruct((NZH, T_L, width), jnp.bfloat16),
        in_specs=[a_spec, a_spec, w_spec, w_spec, w_spec, w_spec],
        out_specs=pl.BlockSpec((NZH, T_L, cols), lambda i: (0, 0, i)),
        compiler_params=params(32),
    )(a_mine, a_other, video_out_w, wv_other, audio_out_w, wa_other)
    summed = lax.all_to_all(shares, "zh", split_axis=0, concat_axis=0, tiled=True)
    proj = jnp.sum(summed.astype(jnp.float32), axis=0)
    video_gate = frame_gate(levels, frame, video_gate_w)
    audio_gate = frame_gate(levels, frame, audio_gate_w)
    video_out = (video_x.astype(jnp.float32) + video_gate * proj[:TV_L]).astype(jnp.bfloat16)
    audio_out = (audio_x.astype(jnp.float32) + audio_gate * proj[TV_L:]).astype(jnp.bfloat16)
    return (video_out, audio_out)


def solution(mesh):
    fine = Mesh(mesh.devices.reshape(NX, NY, NZL, NZH, NC), AXES)
    tokens3 = P(AXES, None, None)
    tokens2 = P(AXES, None)
    weights = P(("zh", "c"), None)
    return jax.shard_map(
        local,
        mesh=fine,
        in_specs=(
            tokens3, tokens3, tokens3, tokens3, tokens3, tokens3,
            tokens2, tokens2, weights, weights, P(), P(), P(), P(), P(AXES),
        ),
        out_specs=(tokens2, tokens2),
        check_vma=False,
    )
```

```python
import functools
import math

import jax
import jax.numpy as jnp
import numpy as np
from jax import lax
from jax.experimental import pallas as pl
from jax.experimental.pallas import tpu as pltpu
from jax.sharding import Mesh
from jax.sharding import PartitionSpec as P

GRID_W = 32
GRID_SHIFT = 5
LEVELS = 1000
FLOW_SHIFT = 5.0
HEADS = 24
HD = 128
NX, NY, NZL, NZH, NC = 4, 4, 2, 4, 2
NZ = NZL * NZH
HPG = HEADS // NZ
TV_L = 48
TA_L = 8
T_L = TV_L + TA_L
ROWS = NZ * T_L
HALF = NZH * T_L
VHALF = NZH * TV_L
CHUNK = 512
STAT = 16
AXES = ("x", "y", "zl", "zh", "c")
VMEM = pl.BlockSpec(memory_space=pltpu.VMEM)
SMEM = pl.BlockSpec(memory_space=pltpu.SMEM)
ANY = pl.BlockSpec(memory_space=pl.ANY)
NT = (((1,), (1,)), ((), ()))


def rope_lanes():
    sixth = HD // 6
    first = HD - 4 * sixth
    partner = np.zeros(HD, np.int32)
    sign = np.zeros(HD, np.float32)
    index = np.zeros(HD, np.float32)
    width_of = np.zeros(HD, np.float32)
    section = np.zeros(HD, np.int32)
    for number, (start, width) in enumerate(
        ((0, first), (first, 2 * sixth), (first + 2 * sixth, 2 * sixth))
    ):
        half = width // 2
        for k in range(half):
            low, high = start + k, start + half + k
            partner[low], partner[high] = high, low
            sign[low], sign[high] = -1.0, 1.0
            index[low] = index[high] = k
            width_of[low] = width_of[high] = width
            section[low] = section[high] = number
    return partner, sign, index, width_of, section


PARTNER, SIGN, INDEX, WIDTH_OF, SECTION = rope_lanes()


def group_of(z):
    return (z % NZH) * NZL + z // NZH


def prep_kernel(
    vpos_in, apos_in, vq_in, vk_in, vv_in, aq_in, ak_in, av_in, table_in, out,
    vpos, apos, vq, vk, vv, aq, ak, av, table, sems,
):
    copies = [
        pltpu.make_async_copy(source, target, sems.at[i])
        for i, (source, target) in enumerate(
            (
                (vpos_in, vpos), (apos_in, apos), (table_in, table), (vq_in, vq), (aq_in, aq),
                (vk_in, vk), (ak_in, ak), (vv_in, vv), (av_in, av),
            )
        )
    ]
    for copy in copies:
        copy.start()
    rank = jnp.int32(0)
    for name, size in zip(AXES, (NX, NY, NZL, NZH, NC)):
        rank = rank * size + lax.axis_index(name)
    per_frame = NX * NY * NZ * NC // vpos_in.shape[0]
    frame = lax.div(rank, jnp.int32(per_frame))
    start = lax.rem(rank, jnp.int32(per_frame)) * TV_L
    row_v = lax.broadcasted_iota(jnp.int32, (TV_L, HD), 0)
    row_a = lax.broadcasted_iota(jnp.int32, (TA_L, HD), 0)
    within = start + row_v
    high = within >> GRID_SHIFT
    wide = within & (GRID_W - 1)
    for copy in copies[0:3]:
        copy.wait()
    section_v = jnp.broadcast_to(table[2:3, :], (TV_L, HD))
    place_v = jnp.where(
        section_v == 0.0,
        vpos[frame].astype(jnp.float32),
        jnp.where(section_v == 1.0, high.astype(jnp.float32), wide.astype(jnp.float32)),
    )
    place_a = jnp.zeros((TA_L, HD), jnp.int32)
    for i in range(TA_L):
        place_a = jnp.where(row_a == i, apos[i], place_a)
    section_a = jnp.broadcast_to(table[2:3, :], (TA_L, HD))
    place_a = jnp.where(section_a == 0.0, place_a.astype(jnp.float32), 0.0)
    turns = []
    for place in (place_v, place_a):
        angles = place * table[0:1, :]
        turns.append((jnp.cos(angles), jnp.sin(angles) * table[1:2, :]))
    perm = table[8 : 8 + HD, :].astype(jnp.bfloat16)

    def turn(ref, cos_sin, gain):
        n, heads, hd = ref.shape
        cos, sin = cos_sin[0] * gain, cos_sin[1] * gain
        u = jnp.swapaxes(ref[...], 0, 1)
        other = jnp.dot(
            u.reshape(heads * n, hd), perm, preferred_element_type=jnp.float32
        ).reshape(heads, n, hd)
        return (u.astype(jnp.float32) * cos[None] + other * sin[None]).astype(jnp.bfloat16)

    scale = math.log2(math.e) / math.sqrt(HD)
    for t, (video, audio, gain) in enumerate(((vq, aq, scale), (vk, ak, 1.0), (vv, av, None))):
        for copy in copies[3 + 2 * t : 5 + 2 * t]:
            copy.wait()
        if gain is None:
            video, audio = jnp.swapaxes(video[...], 0, 1), jnp.swapaxes(audio[...], 0, 1)
        else:
            video, audio = turn(video, turns[0], gain), turn(audio, turns[1], gain)
        for z in range(NZ):
            for h in range(HPG):
                out[z, t, h, 0:TV_L, :] = video[group_of(z) * HPG + h]
                out[z, t, h, TV_L:T_L, :] = audio[group_of(z) * HPG + h]


def arrange_kernel(got, q_out, kv_out):
    for z in range(NZ):
        zl, zh = z // NZH, z % NZH
        v_at = zl * HALF + zh * TV_L
        a_at = zl * HALF + VHALF + zh * TA_L
        for h in range(HPG):
            q_out[h, v_at : v_at + TV_L, :] = got[z, 0, h, 0:TV_L, :]
            q_out[h, a_at : a_at + TA_L, :] = got[z, 0, h, TV_L:T_L, :]
            for t in range(2):
                kv_out[t, h, v_at : v_at + TV_L, :] = got[z, 1 + t, h, 0:TV_L, :]
                kv_out[t, h, a_at : a_at + TA_L, :] = got[z, 1 + t, h, TV_L:T_L, :]


def chunk_starts():
    return [min(at, ROWS - HD) for at in range(0, ROWS, HD)]


def stat_tile(level):
    row = lax.broadcasted_iota(jnp.int32, (STAT, HD), 0)
    flat = jnp.zeros((STAT, HD), jnp.float32)
    for g, at in enumerate(chunk_starts()):
        line = jnp.transpose(level[at : at + HD, :])[0:1, :]
        flat = jnp.where((row & 3) == g, line, flat)
    high = flat.astype(jnp.bfloat16).astype(jnp.float32)
    middle = (flat - high).astype(jnp.bfloat16).astype(jnp.float32)
    low = flat - high - middle
    tile = jnp.where(row < 4, high, jnp.where(row < 8, middle, jnp.where(row < 12, low, 0.0)))
    return tile.astype(jnp.bfloat16)


def attend_heads(queries, keys, values, out, ready):
    n_keys = keys.shape[1]
    cuts = [(at, min(CHUNK, n_keys - at)) for at in range(0, n_keys, CHUNK)]
    for head in range(HPG):
        ready(head)
        rows = queries[head]

        def scores(cut):
            at, size = cut
            return lax.dot_general(
                rows, keys[head, at : at + size, :], NT, preferred_element_type=jnp.float32
            )

        s = scores(cuts[0])
        peak = total = None
        for number, (at, size) in enumerate(cuts):
            coming = scores(cuts[number + 1]) if number + 1 < len(cuts) else None
            slabs = [s[:, g : g + HD] for g in range(0, size, HD)]
            top = jnp.max(functools.reduce(jnp.maximum, slabs), axis=1, keepdims=True)
            top = jnp.broadcast_to(top, (ROWS, HD))
            if peak is not None:
                top = jnp.maximum(peak, top)
            weights = jnp.concatenate(
                [jnp.exp2(slab - top).astype(jnp.bfloat16) for slab in slabs], axis=1
            )
            ones = jnp.ones((size, HD), jnp.bfloat16)
            new = jnp.dot(
                weights,
                jnp.concatenate([values[head, at : at + size, :], ones], axis=1),
                preferred_element_type=jnp.float32,
            )
            if total is None:
                total = new
            else:
                factor = jnp.exp2(peak - top)
                total = total * jnp.concatenate([factor, factor], axis=1) + new
            peak, s = top, coming
        mass = total[:, HD : 2 * HD]
        at = head * (ROWS + STAT)
        out[at : at + ROWS, :] = (total[:, 0:HD] / mass).astype(jnp.bfloat16)
        out[at + ROWS : at + ROWS + STAT, :] = stat_tile(peak + jnp.log2(mass))


def first_kernel(n_pair, n_split, *refs):
    queries = refs[0]
    pairs, splits = refs[1 : 1 + n_pair], refs[1 + n_pair : 1 + n_pair + 2 * n_split]
    out, keys, values, sems = refs[1 + n_pair + 2 * n_split :]
    n_kv = n_pair + n_split
    copies = []
    for h in range(HPG):
        for a in range(n_kv):
            if a < n_pair:
                k_from, v_from = pairs[a].at[0, h], pairs[a].at[1, h]
            else:
                k_from, v_from = (ref.at[h] for ref in splits[2 * (a - n_pair) :][:2])
            place = pl.ds(a * ROWS, ROWS)
            at = 2 * (h * n_kv + a)
            copies.append(pltpu.make_async_copy(k_from, keys.at[h, place, :], sems.at[at]))
            copies.append(pltpu.make_async_copy(v_from, values.at[h, place, :], sems.at[at + 1]))
    for copy in copies:
        copy.start()

    def ready(head):
        for copy in copies[2 * head * n_kv : 2 * (head + 1) * n_kv]:
            copy.wait()

    attend_heads(queries, keys, values, out, ready)


def next_kernel(queries, keys, values, out):
    attend_heads(queries, keys, values, out, lambda head: None)


def attention(queries, pairs, splits, packed):
    n_pair, n_split = len(pairs), len(splits) // 2
    n_keys = NX * NC * ROWS
    out = jax.ShapeDtypeStruct((HPG * (ROWS + STAT), HD), jnp.bfloat16)
    kv = jax.ShapeDtypeStruct((HPG, n_keys, HD), jnp.bfloat16)
    cost = pl.CostEstimate(
        flops=16 * HPG * ROWS * n_keys * HD,
        bytes_accessed=8 << 20,
        transcendentals=HPG * ROWS * n_keys,
    )
    if packed is None:
        return pl.pallas_call(
            functools.partial(first_kernel, n_pair, n_split),
            out_shape=(out, kv, kv),
            in_specs=[VMEM] + [ANY] * (n_pair + 2 * n_split),
            out_specs=(VMEM, VMEM, VMEM),
            scratch_shapes=[pltpu.SemaphoreType.DMA((2 * HPG * (n_pair + n_split),))],
            compiler_params=params(32),
            cost_estimate=cost,
        )(queries, *pairs, *splits)
    return pl.pallas_call(
        next_kernel,
        out_shape=out,
        in_specs=[VMEM] * 3,
        out_specs=VMEM,
        compiler_params=params(32),
        cost_estimate=cost,
    )(queries, *packed)


def merge_kernel(zl_ref, o0, o1, o2, o3, keep, send, merged):
    parts = (o0, o1, o2, o3)
    for h in range(HPG):
        at = h * (ROWS + STAT)
        levels = []
        for part in parts:
            tile = part[at + ROWS : at + ROWS + STAT, :].astype(jnp.float32)
            levels.append(tile[0:4, :] + tile[4:8, :] + tile[8:12, :])
        peak = functools.reduce(jnp.maximum, levels)
        shares = [jnp.exp2(level - peak) for level in levels]
        mass = functools.reduce(jnp.add, shares)
        shares = [share / mass for share in shares]
        flat = jnp.concatenate(shares + [jnp.zeros((HD - 4 * NY, HD), jnp.float32)], axis=0)
        turned = jnp.transpose(flat)
        done = 0
        for g, start in enumerate(chunk_starts()):
            total = None
            for s, part in enumerate(parts):
                share = turned[done - start : HD, 4 * s + g : 4 * s + g + 1]
                rows = part[at + done : at + start + HD, :].astype(jnp.float32)
                total = rows * share if total is None else total + rows * share
            merged[done : start + HD, h * HD : (h + 1) * HD] = total.astype(jnp.bfloat16)
            done = start + HD
    zl = zl_ref[0]
    keep[...] = merged[pl.ds(pl.multiple_of(zl * HALF, 32), HALF), :]
    send[...] = merged[pl.ds(pl.multiple_of((1 - zl) * HALF, 32), HALF), :]


def project_kernel(a_mine, a_other, wv_mine, wv_other, wa_mine, wa_other, out):
    def product(rows, mine, other):
        return (
            jnp.dot(a_mine[rows, :], mine[...], preferred_element_type=jnp.float32)
            + jnp.dot(a_other[rows, :], other[...], preferred_element_type=jnp.float32)
        ).astype(jnp.bfloat16)

    video = product(slice(0, VHALF), wv_mine, wv_other)
    audio = product(slice(VHALF, HALF), wa_mine, wa_other)
    for zh in range(NZH):
        out[zh, 0:TV_L, :] = video[zh * TV_L : (zh + 1) * TV_L, :]
        out[zh, TV_L:T_L, :] = audio[zh * TA_L : (zh + 1) * TA_L, :]


def params(mib):
    return pltpu.CompilerParams(vmem_limit_bytes=mib << 20)


def shift(array, axis, step, size):
    return lax.ppermute(array, axis, [(i, (i + step) % size) for i in range(size)])


def frame_gate(levels, frame, gate_w):
    level = lax.dynamic_slice(levels, (frame,), (1,)).astype(jnp.float32)
    level_frac = (level + 1.0) / LEVELS
    timestep = 1000.0 * FLOW_SHIFT * level_frac / (1.0 + (FLOW_SHIFT - 1.0) * level_frac)
    half_emb = gate_w.shape[0] // 2
    frequency = jnp.exp(-math.log(10000.0) * jnp.arange(half_emb, dtype=jnp.float32) / half_emb)
    angles = timestep[:, None] * frequency[None, :]
    embedding = jnp.concatenate([jnp.cos(angles), jnp.sin(angles)], axis=1)
    return jnp.dot(
        embedding,
        gate_w.astype(jnp.float32),
        precision=lax.Precision.HIGHEST,
        preferred_element_type=jnp.float32,
    )


def local(
    video_q, video_k, video_v, audio_q, audio_k, audio_v, video_x, audio_x,
    video_out_w, audio_out_w, video_gate_w, audio_gate_w, levels, video_pos, audio_pos,
):
    width = HEADS * HD
    rank = lax.axis_index(AXES)
    frame = rank // (NX * NY * NZ * NC // video_pos.shape[0])
    frequency = 10000.0 ** (-(INDEX * np.float32(2.0)) / WIDTH_OF)
    table = jnp.asarray(
        np.concatenate(
            [
                np.stack([frequency, SIGN, SECTION]),
                np.zeros((5, HD)),
                np.arange(HD)[:, None] == PARTNER[None, :],
            ]
        ).astype(np.float32)
    )
    heads = (video_q, video_k, video_v, audio_q, audio_k, audio_v)
    packed = pl.pallas_call(
        prep_kernel,
        out_shape=jax.ShapeDtypeStruct((NZ, 3, HPG, T_L, HD), jnp.bfloat16),
        in_specs=[ANY] * 9,
        out_specs=VMEM,
        scratch_shapes=[
            pltpu.SMEM(video_pos.shape, jnp.int32),
            pltpu.SMEM(audio_pos.shape, jnp.int32),
            *(pltpu.VMEM(array.shape, jnp.bfloat16) for array in heads),
            pltpu.VMEM(table.shape, jnp.float32),
            pltpu.SemaphoreType.DMA((9,)),
        ],
        compiler_params=params(60),
    )(video_pos, audio_pos, *heads, table)
    got = lax.all_to_all(packed, ("zl", "zh"), split_axis=0, concat_axis=0, tiled=True)
    q_mine, kv_mine = pl.pallas_call(
        arrange_kernel,
        out_shape=(
            jax.ShapeDtypeStruct((HPG, ROWS, HD), jnp.bfloat16),
            jax.ShapeDtypeStruct((2, HPG, ROWS, HD), jnp.bfloat16),
        ),
        in_specs=[VMEM],
        out_specs=(VMEM, VMEM),
        compiler_params=params(32),
    )(got)

    kv_left = shift(kv_mine, "x", 1, NX)
    kv_right = shift(kv_mine, "x", NX - 1, NX)
    steps = (1, NY - 1, 2)
    q_far = [shift(q_mine, "y", step, NY) for step in steps]
    kv_left, kv_right, kv_held = lax.optimization_barrier((kv_left, kv_right, kv_mine))
    k_far = shift(kv_left[0], "x", 1, NX)
    v_far = shift(kv_right[1], "x", NX - 1, NX)
    pairs = [kv_held, kv_left, kv_right]
    pairs = pairs + [shift(kv, "c", 1, NC) for kv in pairs]
    splits = [k_far, v_far, shift(k_far, "c", 1, NC), shift(v_far, "c", 1, NC)]
    wv_other = shift(video_out_w, "c", 1, NC)
    wa_other = shift(audio_out_w, "c", 1, NC)

    partial, keys, values = attention(q_far[0], pairs, splits, None)
    back = [shift(partial, "y", NY - steps[0], NY)]
    queries, partial = lax.optimization_barrier((q_far[1], partial))
    partial = attention(queries, (), (), (keys, values))
    back.append(shift(partial, "y", NY - steps[1], NY))
    queries, partial, back[0] = lax.optimization_barrier((q_far[2], partial, back[0]))
    partial = attention(queries, (), (), (keys, values))
    back.append(shift(partial, "y", NY - steps[2], NY))
    queries, partial, back[1] = lax.optimization_barrier((q_mine, partial, back[1]))
    back = [attention(queries, (), (), (keys, values))] + back
    zl = lax.axis_index("zl")
    c = lax.axis_index("c")
    a_shape = jax.ShapeDtypeStruct((HALF, HPG * HD), jnp.bfloat16)
    keep, send = pl.pallas_call(
        merge_kernel,
        out_shape=(a_shape, a_shape),
        in_specs=[SMEM] + [VMEM] * NY,
        out_specs=(VMEM, VMEM),
        scratch_shapes=[pltpu.VMEM((ROWS, HPG * HD), jnp.bfloat16)],
        compiler_params=params(32),
    )(jnp.full((1,), zl, jnp.int32), *back)
    came = shift(send, "zl", 1, NZL)
    same = zl == c
    a_mine = jnp.where(same, keep, came)
    a_other = jnp.where(same, came, keep)

    cols = 768
    a_spec = pl.BlockSpec((HALF, HPG * HD), lambda i: (0, 0))
    w_spec = pl.BlockSpec((HPG * HD, cols), lambda i: (0, i))
    shares = pl.pallas_call(
        project_kernel,
        grid=(width // cols,),
        out_shape=jax.ShapeDtypeStruct((NZH, T_L, width), jnp.bfloat16),
        in_specs=[a_spec, a_spec, w_spec, w_spec, w_spec, w_spec],
        out_specs=pl.BlockSpec((NZH, T_L, cols), lambda i: (0, 0, i)),
        compiler_params=params(32),
    )(a_mine, a_other, video_out_w, wv_other, audio_out_w, wa_other)
    summed = lax.all_to_all(shares, "zh", split_axis=0, concat_axis=0, tiled=True)
    proj = jnp.sum(summed.astype(jnp.float32), axis=0)
    video_gate = frame_gate(levels, frame, video_gate_w)
    audio_gate = frame_gate(levels, frame, audio_gate_w)
    video_out = (video_x.astype(jnp.float32) + video_gate * proj[:TV_L]).astype(jnp.bfloat16)
    audio_out = (audio_x.astype(jnp.float32) + audio_gate * proj[TV_L:]).astype(jnp.bfloat16)
    return (video_out, audio_out)


def solution(mesh):
    fine = Mesh(mesh.devices.reshape(NX, NY, NZL, NZH, NC), AXES)
    tokens3 = P(AXES, None, None)
    tokens2 = P(AXES, None)
    weights = P(("zh", "c"), None)
    return jax.shard_map(
        local,
        mesh=fine,
        in_specs=(
            tokens3, tokens3, tokens3, tokens3, tokens3, tokens3,
            tokens2, tokens2, weights, weights, P(), P(), P(), P(), P(AXES),
        ),
        out_specs=(tokens2, tokens2),
        check_vma=False,
    )
```

```python
import functools
import math

import jax
import jax.numpy as jnp
import numpy as np
from jax import lax
from jax.experimental import pallas as pl
from jax.experimental.pallas import tpu as pltpu
from jax.sharding import Mesh
from jax.sharding import PartitionSpec as P

GRID_W = 32
GRID_SHIFT = 5
LEVELS = 1000
FLOW_SHIFT = 5.0
HEADS = 24
HD = 128
NX, NY, NZL, NZH, NC = 4, 4, 2, 4, 2
NZ = NZL * NZH
HPG = HEADS // NZ
TV_L = 48
TA_L = 8
T_L = TV_L + TA_L
ROWS = NZ * T_L
HALF = NZH * T_L
VHALF = NZH * TV_L
CHUNK = 512
STAT = 16
AXES = ("x", "y", "zl", "zh", "c")
VMEM = pl.BlockSpec(memory_space=pltpu.VMEM)
SMEM = pl.BlockSpec(memory_space=pltpu.SMEM)
ANY = pl.BlockSpec(memory_space=pl.ANY)
NT = (((1,), (1,)), ((), ()))


def rope_lanes():
    sixth = HD // 6
    first = HD - 4 * sixth
    partner = np.zeros(HD, np.int32)
    sign = np.zeros(HD, np.float32)
    index = np.zeros(HD, np.float32)
    width_of = np.zeros(HD, np.float32)
    section = np.zeros(HD, np.int32)
    for number, (start, width) in enumerate(
        ((0, first), (first, 2 * sixth), (first + 2 * sixth, 2 * sixth))
    ):
        half = width // 2
        for k in range(half):
            low, high = start + k, start + half + k
            partner[low], partner[high] = high, low
            sign[low], sign[high] = -1.0, 1.0
            index[low] = index[high] = k
            width_of[low] = width_of[high] = width
            section[low] = section[high] = number
    return partner, sign, index, width_of, section


PARTNER, SIGN, INDEX, WIDTH_OF, SECTION = rope_lanes()


def group_of(z):
    return (z % NZH) * NZL + z // NZH


def prep_kernel(
    vpos_in, apos_in, vq_in, vk_in, vv_in, aq_in, ak_in, av_in, table_in, out,
    vpos, apos, vq, vk, vv, aq, ak, av, table, sems,
):
    copies = [
        pltpu.make_async_copy(source, target, sems.at[i])
        for i, (source, target) in enumerate(
            (
                (vpos_in, vpos), (apos_in, apos), (table_in, table), (vq_in, vq), (aq_in, aq),
                (vk_in, vk), (ak_in, ak), (vv_in, vv), (av_in, av),
            )
        )
    ]
    for copy in copies:
        copy.start()
    rank = jnp.int32(0)
    for name, size in zip(AXES, (NX, NY, NZL, NZH, NC)):
        rank = rank * size + lax.axis_index(name)
    per_frame = NX * NY * NZ * NC // vpos_in.shape[0]
    frame = lax.div(rank, jnp.int32(per_frame))
    start = lax.rem(rank, jnp.int32(per_frame)) * TV_L
    row_v = lax.broadcasted_iota(jnp.int32, (TV_L, HD), 0)
    row_a = lax.broadcasted_iota(jnp.int32, (TA_L, HD), 0)
    within = start + row_v
    high = within >> GRID_SHIFT
    wide = within & (GRID_W - 1)
    for copy in copies[0:3]:
        copy.wait()
    section_v = jnp.broadcast_to(table[2:3, :], (TV_L, HD))
    place_v = jnp.where(
        section_v == 0.0,
        vpos[frame].astype(jnp.float32),
        jnp.where(section_v == 1.0, high.astype(jnp.float32), wide.astype(jnp.float32)),
    )
    place_a = jnp.zeros((TA_L, HD), jnp.int32)
    for i in range(TA_L):
        place_a = jnp.where(row_a == i, apos[i], place_a)
    section_a = jnp.broadcast_to(table[2:3, :], (TA_L, HD))
    place_a = jnp.where(section_a == 0.0, place_a.astype(jnp.float32), 0.0)
    turns = []
    for place in (place_v, place_a):
        angles = place * table[0:1, :]
        turns.append((jnp.cos(angles), jnp.sin(angles) * table[1:2, :]))
    perm = table[8 : 8 + HD, :].astype(jnp.bfloat16)

    def turn(ref, cos_sin, gain):
        n, heads, hd = ref.shape
        cos, sin = cos_sin[0] * gain, cos_sin[1] * gain
        u = jnp.swapaxes(ref[...], 0, 1)
        other = jnp.dot(
            u.reshape(heads * n, hd), perm, preferred_element_type=jnp.float32
        ).reshape(heads, n, hd)
        return (u.astype(jnp.float32) * cos[None] + other * sin[None]).astype(jnp.bfloat16)

    scale = math.log2(math.e) / math.sqrt(HD)
    for t, (video, audio, gain) in enumerate(((vq, aq, scale), (vk, ak, 1.0), (vv, av, None))):
        for copy in copies[3 + 2 * t : 5 + 2 * t]:
            copy.wait()
        if gain is None:
            video, audio = jnp.swapaxes(video[...], 0, 1), jnp.swapaxes(audio[...], 0, 1)
        else:
            video, audio = turn(video, turns[0], gain), turn(audio, turns[1], gain)
        for z in range(NZ):
            for h in range(HPG):
                out[z, t, h, 0:TV_L, :] = video[group_of(z) * HPG + h]
                out[z, t, h, TV_L:T_L, :] = audio[group_of(z) * HPG + h]


def arrange_kernel(got, q_out, kv_out):
    here = lax.axis_index("zh")
    for zl in range(NZL):
        for r in range(NZH):
            z = zl * NZH + lax.rem(here + r, NZH)
            v_at = zl * HALF + r * TV_L
            a_at = zl * HALF + VHALF + r * TA_L
            for h in range(HPG):
                q_out[h, v_at : v_at + TV_L, :] = got[z, 0, h, 0:TV_L, :]
                q_out[h, a_at : a_at + TA_L, :] = got[z, 0, h, TV_L:T_L, :]
                for t in range(2):
                    kv_out[t, h, v_at : v_at + TV_L, :] = got[z, 1 + t, h, 0:TV_L, :]
                    kv_out[t, h, a_at : a_at + TA_L, :] = got[z, 1 + t, h, TV_L:T_L, :]


def chunk_starts():
    return [min(at, ROWS - HD) for at in range(0, ROWS, HD)]


def stat_tile(level):
    row = lax.broadcasted_iota(jnp.int32, (STAT, HD), 0)
    flat = jnp.zeros((STAT, HD), jnp.float32)
    for g, at in enumerate(chunk_starts()):
        line = jnp.transpose(level[at : at + HD, :])[0:1, :]
        flat = jnp.where((row & 3) == g, line, flat)
    high = flat.astype(jnp.bfloat16).astype(jnp.float32)
    middle = (flat - high).astype(jnp.bfloat16).astype(jnp.float32)
    low = flat - high - middle
    tile = jnp.where(row < 4, high, jnp.where(row < 8, middle, jnp.where(row < 12, low, 0.0)))
    return tile.astype(jnp.bfloat16)


def attend_heads(queries, keys, values, out, ready):
    n_keys = keys.shape[1]
    cuts = [(at, min(CHUNK, n_keys - at)) for at in range(0, n_keys, CHUNK)]
    for head in range(HPG):
        ready(head)
        rows = queries[head]

        def scores(cut):
            at, size = cut
            return lax.dot_general(
                rows, keys[head, at : at + size, :], NT, preferred_element_type=jnp.float32
            )

        s = scores(cuts[0])
        peak = total = None
        for number, (at, size) in enumerate(cuts):
            coming = scores(cuts[number + 1]) if number + 1 < len(cuts) else None
            slabs = [s[:, g : g + HD] for g in range(0, size, HD)]
            top = jnp.max(functools.reduce(jnp.maximum, slabs), axis=1, keepdims=True)
            top = jnp.broadcast_to(top, (ROWS, HD))
            if peak is not None:
                top = jnp.maximum(peak, top)
            weights = jnp.concatenate(
                [jnp.exp2(slab - top).astype(jnp.bfloat16) for slab in slabs], axis=1
            )
            ones = jnp.ones((size, HD), jnp.bfloat16)
            new = jnp.dot(
                weights,
                jnp.concatenate([values[head, at : at + size, :], ones], axis=1),
                preferred_element_type=jnp.float32,
            )
            if total is None:
                total = new
            else:
                factor = jnp.exp2(peak - top)
                total = total * jnp.concatenate([factor, factor], axis=1) + new
            peak, s = top, coming
        mass = total[:, HD : 2 * HD]
        at = head * (ROWS + STAT)
        out[at : at + ROWS, :] = (total[:, 0:HD] / mass).astype(jnp.bfloat16)
        out[at + ROWS : at + ROWS + STAT, :] = stat_tile(peak + jnp.log2(mass))


def query_copies(queries, rows, sems):
    return [
        pltpu.make_async_copy(queries.at[h], rows.at[h], sems.at[h]) for h in range(HPG)
    ]


def first_kernel(n_pair, n_split, *refs):
    queries = refs[0]
    pairs, splits = refs[1 : 1 + n_pair], refs[1 + n_pair : 1 + n_pair + 2 * n_split]
    out, keys, values, rows, sems, row_sems = refs[1 + n_pair + 2 * n_split :]
    n_kv = n_pair + n_split
    row_copies = query_copies(queries, rows, row_sems)
    copies = []
    for h in range(HPG):
        for a in range(n_kv):
            if a < n_pair:
                k_from, v_from = pairs[a].at[0, h], pairs[a].at[1, h]
            else:
                k_from, v_from = (ref.at[h] for ref in splits[2 * (a - n_pair) :][:2])
            place = pl.ds(a * ROWS, ROWS)
            at = 2 * (h * n_kv + a)
            copies.append(pltpu.make_async_copy(k_from, keys.at[h, place, :], sems.at[at]))
            copies.append(pltpu.make_async_copy(v_from, values.at[h, place, :], sems.at[at + 1]))
    for h in range(HPG):
        row_copies[h].start()
        for copy in copies[2 * h * n_kv : 2 * (h + 1) * n_kv]:
            copy.start()

    def ready(head):
        row_copies[head].wait()
        for copy in copies[2 * head * n_kv : 2 * (head + 1) * n_kv]:
            copy.wait()

    attend_heads(rows, keys, values, out, ready)


def next_kernel(queries, keys, values, out, rows, row_sems):
    row_copies = query_copies(queries, rows, row_sems)
    for copy in row_copies:
        copy.start()
    attend_heads(rows, keys, values, out, lambda head: row_copies[head].wait())


def attention(queries, pairs, splits, packed):
    n_pair, n_split = len(pairs), len(splits) // 2
    n_keys = NX * NC * ROWS
    out = jax.ShapeDtypeStruct((HPG * (ROWS + STAT), HD), jnp.bfloat16)
    kv = jax.ShapeDtypeStruct((HPG, n_keys, HD), jnp.bfloat16)
    rows = pltpu.VMEM((HPG, ROWS, HD), jnp.bfloat16)
    row_sems = pltpu.SemaphoreType.DMA((HPG,))
    cost = pl.CostEstimate(
        flops=16 * HPG * ROWS * n_keys * HD,
        bytes_accessed=8 << 20,
        transcendentals=HPG * ROWS * n_keys,
    )
    if packed is None:
        return pl.pallas_call(
            functools.partial(first_kernel, n_pair, n_split),
            out_shape=(out, kv, kv),
            in_specs=[ANY] * (1 + n_pair + 2 * n_split),
            out_specs=(VMEM, VMEM, VMEM),
            scratch_shapes=[
                rows, pltpu.SemaphoreType.DMA((2 * HPG * (n_pair + n_split),)), row_sems,
            ],
            compiler_params=params(32),
            cost_estimate=cost,
        )(queries, *pairs, *splits)
    return pl.pallas_call(
        next_kernel,
        out_shape=out,
        in_specs=[ANY, VMEM, VMEM],
        out_specs=VMEM,
        scratch_shapes=[rows, row_sems],
        compiler_params=params(32),
        cost_estimate=cost,
    )(queries, *packed)


def merge_kernel(zl_ref, o0, o1, o2, o3, keep, send, merged):
    parts = (o0, o1, o2, o3)
    for h in range(HPG):
        at = h * (ROWS + STAT)
        levels = []
        for part in parts:
            tile = part[at + ROWS : at + ROWS + STAT, :].astype(jnp.float32)
            levels.append(tile[0:4, :] + tile[4:8, :] + tile[8:12, :])
        peak = functools.reduce(jnp.maximum, levels)
        shares = [jnp.exp2(level - peak) for level in levels]
        mass = functools.reduce(jnp.add, shares)
        shares = [share / mass for share in shares]
        flat = jnp.concatenate(shares + [jnp.zeros((HD - 4 * NY, HD), jnp.float32)], axis=0)
        turned = jnp.transpose(flat)
        done = 0
        for g, start in enumerate(chunk_starts()):
            total = None
            for s, part in enumerate(parts):
                share = turned[done - start : HD, 4 * s + g : 4 * s + g + 1]
                rows = part[at + done : at + start + HD, :].astype(jnp.float32)
                total = rows * share if total is None else total + rows * share
            merged[done : start + HD, h * HD : (h + 1) * HD] = total.astype(jnp.bfloat16)
            done = start + HD
    zl = zl_ref[0]
    keep[...] = merged[pl.ds(pl.multiple_of(zl * HALF, 32), HALF), :]
    send[...] = merged[pl.ds(pl.multiple_of((1 - zl) * HALF, 32), HALF), :]


def project_kernel(a_mine, a_other, wv_mine, wv_other, wa_mine, wa_other, own, *sides):
    def product(rows, mine, other):
        return (
            jnp.dot(a_mine[rows, :], mine[...], preferred_element_type=jnp.float32)
            + jnp.dot(a_other[rows, :], other[...], preferred_element_type=jnp.float32)
        ).astype(jnp.bfloat16)

    video = product(slice(0, VHALF), wv_mine, wv_other)
    audio = product(slice(VHALF, HALF), wa_mine, wa_other)

    def put(ref, r):
        ref[0:TV_L, :] = video[r * TV_L : (r + 1) * TV_L, :]
        ref[TV_L:T_L, :] = audio[r * TA_L : (r + 1) * TA_L, :]

    put(own, 0)
    lower = pl.program_id(0) < pl.num_programs(0) // 2

    @pl.when(lower)
    def _():
        for r in range(1, NZH):
            put(sides[2 * (r - 1)], r)

    @pl.when(jnp.logical_not(lower))
    def _():
        for r in range(1, NZH):
            put(sides[2 * (r - 1) + 1], r)


def finish_kernel(own, a_one, a_two, b_one, b_two, xv, xa, gv, ga, out_v, out_a):
    half = a_one.shape[1]
    for at, one, two in ((0, a_one, a_two), (half, b_one, b_two)):
        cols = slice(at, at + half)
        proj = (
            own[:, cols].astype(jnp.float32)
            + one[...].astype(jnp.float32)
            + two[...].astype(jnp.float32)
        )
        out_v[:, cols] = (
            xv[:, cols].astype(jnp.float32) + gv[:, cols] * proj[0:TV_L, :]
        ).astype(jnp.bfloat16)
        out_a[:, cols] = (
            xa[:, cols].astype(jnp.float32) + ga[:, cols] * proj[TV_L:T_L, :]
        ).astype(jnp.bfloat16)


def params(mib):
    return pltpu.CompilerParams(vmem_limit_bytes=mib << 20)


def shift(array, axis, step, size):
    return lax.ppermute(array, axis, [(i, (i + step) % size) for i in range(size)])


def frame_gate(levels, frame, gate_w):
    level = lax.dynamic_slice(levels, (frame,), (1,)).astype(jnp.float32)
    level_frac = (level + 1.0) / LEVELS
    timestep = 1000.0 * FLOW_SHIFT * level_frac / (1.0 + (FLOW_SHIFT - 1.0) * level_frac)
    half_emb = gate_w.shape[0] // 2
    frequency = jnp.exp(-math.log(10000.0) * jnp.arange(half_emb, dtype=jnp.float32) / half_emb)
    angles = timestep[:, None] * frequency[None, :]
    embedding = jnp.concatenate([jnp.cos(angles), jnp.sin(angles)], axis=1)
    return jnp.dot(
        embedding,
        gate_w.astype(jnp.float32),
        precision=lax.Precision.HIGHEST,
        preferred_element_type=jnp.float32,
    )


def local(
    video_q, video_k, video_v, audio_q, audio_k, audio_v, video_x, audio_x,
    video_out_w, audio_out_w, video_gate_w, audio_gate_w, levels, video_pos, audio_pos,
):
    width = HEADS * HD
    rank = lax.axis_index(AXES)
    frame = rank // (NX * NY * NZ * NC // video_pos.shape[0])
    frequency = 10000.0 ** (-(INDEX * np.float32(2.0)) / WIDTH_OF)
    table = jnp.asarray(
        np.concatenate(
            [
                np.stack([frequency, SIGN, SECTION]),
                np.zeros((5, HD)),
                np.arange(HD)[:, None] == PARTNER[None, :],
            ]
        ).astype(np.float32)
    )
    heads = (video_q, video_k, video_v, audio_q, audio_k, audio_v)
    packed = pl.pallas_call(
        prep_kernel,
        out_shape=jax.ShapeDtypeStruct((NZ, 3, HPG, T_L, HD), jnp.bfloat16),
        in_specs=[ANY] * 9,
        out_specs=VMEM,
        scratch_shapes=[
            pltpu.SMEM(video_pos.shape, jnp.int32),
            pltpu.SMEM(audio_pos.shape, jnp.int32),
            *(pltpu.VMEM(array.shape, jnp.bfloat16) for array in heads),
            pltpu.VMEM(table.shape, jnp.float32),
            pltpu.SemaphoreType.DMA((9,)),
        ],
        compiler_params=params(60),
    )(video_pos, audio_pos, *heads, table)
    got = lax.all_to_all(packed, ("zl", "zh"), split_axis=0, concat_axis=0, tiled=True)
    q_mine, kv_mine = pl.pallas_call(
        arrange_kernel,
        out_shape=(
            jax.ShapeDtypeStruct((HPG, ROWS, HD), jnp.bfloat16),
            jax.ShapeDtypeStruct((2, HPG, ROWS, HD), jnp.bfloat16),
        ),
        in_specs=[VMEM],
        out_specs=(VMEM, VMEM),
        compiler_params=params(32),
    )(got)

    kv_left = shift(kv_mine, "x", 1, NX)
    kv_right = shift(kv_mine, "x", NX - 1, NX)
    steps = (1, NY - 1, 2)
    q_far = [shift(q_mine, "y", step, NY) for step in steps]
    kv_left, kv_right, kv_held, q_far[0], q_far[1] = lax.optimization_barrier(
        (kv_left, kv_right, kv_mine, q_far[0], q_far[1])
    )
    k_far = shift(kv_left[0], "x", 1, NX)
    v_far = shift(kv_right[1], "x", NX - 1, NX)
    pairs = [kv_held, kv_left, kv_right]
    pairs = pairs + [shift(kv, "c", 1, NC) for kv in pairs]
    splits = [k_far, v_far, shift(k_far, "c", 1, NC), shift(v_far, "c", 1, NC)]

    partial, keys, values = attention(q_far[0], pairs, splits, None)
    partial, video_w, audio_w = lax.optimization_barrier((partial, video_out_w, audio_out_w))
    back = [shift(partial, "y", NY - steps[0], NY)]
    wv_other = shift(video_w, "c", 1, NC)
    wa_other = shift(audio_w, "c", 1, NC)
    queries, partial = lax.optimization_barrier((q_far[1], partial))
    partial = attention(queries, (), (), (keys, values))
    back.append(shift(partial, "y", NY - steps[1], NY))
    queries, partial, back[0] = lax.optimization_barrier((q_far[2], partial, back[0]))
    partial = attention(queries, (), (), (keys, values))
    back.append(shift(partial, "y", NY - steps[2], NY))
    queries, partial, back[1] = lax.optimization_barrier((q_mine, partial, back[1]))
    back = [attention(queries, (), (), (keys, values))] + back
    zl = lax.axis_index("zl")
    c = lax.axis_index("c")
    a_shape = jax.ShapeDtypeStruct((HALF, HPG * HD), jnp.bfloat16)
    keep, send = pl.pallas_call(
        merge_kernel,
        out_shape=(a_shape, a_shape),
        in_specs=[SMEM] + [VMEM] * NY,
        out_specs=(VMEM, VMEM),
        scratch_shapes=[pltpu.VMEM((ROWS, HPG * HD), jnp.bfloat16)],
        compiler_params=params(32),
    )(jnp.full((1,), zl, jnp.int32), *back)
    came = shift(send, "zl", 1, NZL)
    same = zl == c
    a_mine = jnp.where(same, keep, came)
    a_other = jnp.where(same, came, keep)

    cols = 768
    blocks = width // cols
    half = width // 2
    a_spec = pl.BlockSpec((HALF, HPG * HD), lambda i: (0, 0))
    w_spec = pl.BlockSpec((HPG * HD, cols), lambda i: (0, i))
    low_spec = pl.BlockSpec((T_L, cols), lambda i: (0, jnp.minimum(i, blocks // 2 - 1)))
    high_spec = pl.BlockSpec((T_L, cols), lambda i: (0, jnp.maximum(i - blocks // 2, 0)))
    side = jax.ShapeDtypeStruct((T_L, half), jnp.bfloat16)
    own, right_a, right_b, far_a, far_b, left_a, left_b = pl.pallas_call(
        project_kernel,
        grid=(blocks,),
        out_shape=(jax.ShapeDtypeStruct((T_L, width), jnp.bfloat16),) + (side,) * 6,
        in_specs=[a_spec, a_spec, w_spec, w_spec, w_spec, w_spec],
        out_specs=(pl.BlockSpec((T_L, cols), lambda i: (0, i)),) + (low_spec, high_spec) * 3,
        compiler_params=params(60),
    )(a_mine, a_other, video_out_w, wv_other, audio_out_w, wa_other)
    far_a = shift(far_a, "zh", 1, NZH)
    far_b = shift(far_b, "zh", NZH - 1, NZH)
    b_one = shift(right_b, "zh", 1, NZH)
    a_two = shift(left_a, "zh", NZH - 1, NZH)

    def add(one, two):
        return (one.astype(jnp.float32) + two.astype(jnp.float32)).astype(jnp.bfloat16)

    a_one = shift(add(right_a, far_a), "zh", 1, NZH)
    b_two = shift(add(left_b, far_b), "zh", NZH - 1, NZH)
    video_gate = frame_gate(levels, frame, video_gate_w)
    audio_gate = frame_gate(levels, frame, audio_gate_w)
    return tuple(
        pl.pallas_call(
            finish_kernel,
            out_shape=(
                jax.ShapeDtypeStruct(video_x.shape, jnp.bfloat16),
                jax.ShapeDtypeStruct(audio_x.shape, jnp.bfloat16),
            ),
            in_specs=[VMEM] * 9,
            out_specs=(VMEM, VMEM),
            compiler_params=params(32),
        )(own, a_one, a_two, b_one, b_two, video_x, audio_x, video_gate, audio_gate)
    )


def solution(mesh):
    fine = Mesh(mesh.devices.reshape(NX, NY, NZL, NZH, NC), AXES)
    tokens3 = P(AXES, None, None)
    tokens2 = P(AXES, None)
    weights = P(("zh", "c"), None)
    return jax.shard_map(
        local,
        mesh=fine,
        in_specs=(
            tokens3, tokens3, tokens3, tokens3, tokens3, tokens3,
            tokens2, tokens2, weights, weights, P(), P(), P(), P(), P(AXES),
        ),
        out_specs=(tokens2, tokens2),
        check_vma=False,
    )
```

```python
import functools
import math

import jax
import jax.numpy as jnp
import numpy as np
from jax import lax
from jax.experimental import pallas as pl
from jax.experimental.pallas import tpu as pltpu
from jax.sharding import Mesh
from jax.sharding import PartitionSpec as P

GRID_W = 32
GRID_SHIFT = 5
LEVELS = 1000
FLOW_SHIFT = 5.0
HEADS = 24
HD = 128
NX, NY, NZL, NZH, NC = 4, 4, 2, 4, 2
NZ = NZL * NZH
HPG = HEADS // NZ
TV_L = 48
TA_L = 8
T_L = TV_L + TA_L
ROWS = NZ * T_L
HALF = NZH * T_L
VHALF = NZH * TV_L
CHUNK = 512
STAT = 16
AXES = ("x", "y", "zl", "zh", "c")
VMEM = pl.BlockSpec(memory_space=pltpu.VMEM)
SMEM = pl.BlockSpec(memory_space=pltpu.SMEM)
ANY = pl.BlockSpec(memory_space=pl.ANY)
NT = (((1,), (1,)), ((), ()))


def rope_lanes():
    sixth = HD // 6
    first = HD - 4 * sixth
    partner = np.zeros(HD, np.int32)
    sign = np.zeros(HD, np.float32)
    index = np.zeros(HD, np.float32)
    width_of = np.zeros(HD, np.float32)
    section = np.zeros(HD, np.int32)
    for number, (start, width) in enumerate(
        ((0, first), (first, 2 * sixth), (first + 2 * sixth, 2 * sixth))
    ):
        half = width // 2
        for k in range(half):
            low, high = start + k, start + half + k
            partner[low], partner[high] = high, low
            sign[low], sign[high] = -1.0, 1.0
            index[low] = index[high] = k
            width_of[low] = width_of[high] = width
            section[low] = section[high] = number
    return partner, sign, index, width_of, section


PARTNER, SIGN, INDEX, WIDTH_OF, SECTION = rope_lanes()


def prep_kernel(
    vpos_in, apos_in, vq_in, vk_in, vv_in, aq_in, ak_in, av_in, table_in, *refs
):
    outs = refs[0:NZ]
    vpos, apos, vq, vk, vv, aq, ak, av, table, turned_v, turned_a, sems = refs[NZ:]
    copies = [
        pltpu.make_async_copy(source, target, sems.at[i])
        for i, (source, target) in enumerate(
            (
                (vpos_in, vpos), (apos_in, apos), (table_in, table), (vq_in, vq), (aq_in, aq),
                (vk_in, vk), (ak_in, ak), (vv_in, vv), (av_in, av),
            )
        )
    ]
    for copy in copies:
        copy.start()
    rank = jnp.int32(0)
    for name, size in zip(AXES, (NX, NY, NZL, NZH, NC)):
        rank = rank * size + lax.axis_index(name)
    per_frame = NX * NY * NZ * NC // vpos_in.shape[0]
    frame = lax.div(rank, jnp.int32(per_frame))
    start = lax.rem(rank, jnp.int32(per_frame)) * TV_L
    row_v = lax.broadcasted_iota(jnp.int32, (TV_L, HD), 0)
    row_a = lax.broadcasted_iota(jnp.int32, (TA_L, HD), 0)
    within = start + row_v
    high = within >> GRID_SHIFT
    wide = within & (GRID_W - 1)
    for copy in copies[0:3]:
        copy.wait()
    section_v = jnp.broadcast_to(table[2:3, :], (TV_L, HD))
    place_v = jnp.where(
        section_v == 0.0,
        vpos[frame].astype(jnp.float32),
        jnp.where(section_v == 1.0, high.astype(jnp.float32), wide.astype(jnp.float32)),
    )
    place_a = jnp.zeros((TA_L, HD), jnp.int32)
    for i in range(TA_L):
        place_a = jnp.where(row_a == i, apos[i], place_a)
    section_a = jnp.broadcast_to(table[2:3, :], (TA_L, HD))
    place_a = jnp.where(section_a == 0.0, place_a.astype(jnp.float32), 0.0)
    turns = []
    for place in (place_v, place_a):
        angles = place * table[0:1, :]
        turns.append((jnp.cos(angles), jnp.sin(angles) * table[1:2, :]))
    perm = table[8 : 8 + HD, :].astype(jnp.bfloat16)

    def turn(ref, cos_sin, gain):
        n, heads, hd = ref.shape
        cos, sin = cos_sin[0] * gain, cos_sin[1] * gain
        u = jnp.swapaxes(ref[...], 0, 1)
        other = jnp.dot(
            u.reshape(heads * n, hd), perm, preferred_element_type=jnp.float32
        ).reshape(heads, n, hd)
        return (u.astype(jnp.float32) * cos[None] + other * sin[None]).astype(jnp.bfloat16)

    scale = math.log2(math.e) / math.sqrt(HD)
    for t, (video, audio, gain) in enumerate(((vq, aq, scale), (vk, ak, 1.0), (vv, av, None))):
        for copy in copies[3 + 2 * t : 5 + 2 * t]:
            copy.wait()
        if gain is None:
            video, audio = jnp.swapaxes(video[...], 0, 1), jnp.swapaxes(audio[...], 0, 1)
        else:
            video, audio = turn(video, turns[0], gain), turn(audio, turns[1], gain)
        turned_v[t] = video
        turned_a[t] = audio
    here = lax.axis_index("zh") * NZL + lax.axis_index("zl")
    for j in range(NZ):
        first = lax.rem(here + j, NZ) * HPG
        for t in range(3):
            for h in range(HPG):
                outs[j][t, h, 0:TV_L, :] = turned_v[t, first + h]
                outs[j][t, h, TV_L:T_L, :] = turned_a[t, first + h]


def arrange_kernel(*refs):
    q_out, kv_out, got, sems = refs[NZ:]
    copies = [pltpu.make_async_copy(refs[j], got.at[j], sems.at[j]) for j in range(NZ)]
    for copy in copies:
        copy.start()
    my_zh = lax.axis_index("zh")
    here = my_zh * NZL + lax.axis_index("zl")
    for copy in copies:
        copy.wait()
    for zl in range(NZL):
        for r in range(NZH):
            source = lax.rem(my_zh + r, NZH) * NZL + zl
            z = lax.rem(here + NZ - source, NZ)
            v_at = zl * HALF + r * TV_L
            a_at = zl * HALF + VHALF + r * TA_L
            for h in range(HPG):
                q_out[h, v_at : v_at + TV_L, :] = got[z, 0, h, 0:TV_L, :]
                q_out[h, a_at : a_at + TA_L, :] = got[z, 0, h, TV_L:T_L, :]
                for t in range(2):
                    kv_out[t, h, v_at : v_at + TV_L, :] = got[z, 1 + t, h, 0:TV_L, :]
                    kv_out[t, h, a_at : a_at + TA_L, :] = got[z, 1 + t, h, TV_L:T_L, :]


def chunk_starts():
    return [min(at, ROWS - HD) for at in range(0, ROWS, HD)]


def stat_tile(level):
    row = lax.broadcasted_iota(jnp.int32, (STAT, HD), 0)
    flat = jnp.zeros((STAT, HD), jnp.float32)
    for g, at in enumerate(chunk_starts()):
        line = jnp.transpose(level[at : at + HD, :])[0:1, :]
        flat = jnp.where((row & 3) == g, line, flat)
    high = flat.astype(jnp.bfloat16).astype(jnp.float32)
    middle = (flat - high).astype(jnp.bfloat16).astype(jnp.float32)
    low = flat - high - middle
    tile = jnp.where(row < 4, high, jnp.where(row < 8, middle, jnp.where(row < 12, low, 0.0)))
    return tile.astype(jnp.bfloat16)


def attend_heads(queries, keys, values, out, ready):
    n_keys = keys.shape[1]
    cuts = [(at, min(CHUNK, n_keys - at)) for at in range(0, n_keys, CHUNK)]
    for head in range(HPG):
        ready(head)
        rows = queries[head]

        def scores(cut):
            at, size = cut
            return lax.dot_general(
                rows, keys[head, at : at + size, :], NT, preferred_element_type=jnp.float32
            )

        s = scores(cuts[0])
        peak = total = None
        for number, (at, size) in enumerate(cuts):
            coming = scores(cuts[number + 1]) if number + 1 < len(cuts) else None
            slabs = [s[:, g : g + HD] for g in range(0, size, HD)]
            top = jnp.max(functools.reduce(jnp.maximum, slabs), axis=1, keepdims=True)
            top = jnp.broadcast_to(top, (ROWS, HD))
            if peak is not None:
                top = jnp.maximum(peak, top)
            weights = jnp.concatenate(
                [jnp.exp2(slab - top).astype(jnp.bfloat16) for slab in slabs], axis=1
            )
            ones = jnp.ones((size, HD), jnp.bfloat16)
            new = jnp.dot(
                weights,
                jnp.concatenate([values[head, at : at + size, :], ones], axis=1),
                preferred_element_type=jnp.float32,
            )
            if total is None:
                total = new
            else:
                factor = jnp.exp2(peak - top)
                total = total * jnp.concatenate([factor, factor], axis=1) + new
            peak, s = top, coming
        mass = total[:, HD : 2 * HD]
        at = head * (ROWS + STAT)
        out[at : at + ROWS, :] = (total[:, 0:HD] / mass).astype(jnp.bfloat16)
        out[at + ROWS : at + ROWS + STAT, :] = stat_tile(peak + jnp.log2(mass))


def query_copies(queries, rows, sems):
    return [
        pltpu.make_async_copy(queries.at[h], rows.at[h], sems.at[h]) for h in range(HPG)
    ]


def first_kernel(n_pair, n_split, *refs):
    queries = refs[0]
    pairs, splits = refs[1 : 1 + n_pair], refs[1 + n_pair : 1 + n_pair + 2 * n_split]
    out, keys, values, rows, sems, row_sems = refs[1 + n_pair + 2 * n_split :]
    n_kv = n_pair + n_split
    row_copies = query_copies(queries, rows, row_sems)
    copies = []
    for h in range(HPG):
        for a in range(n_kv):
            if a < n_pair:
                k_from, v_from = pairs[a].at[0, h], pairs[a].at[1, h]
            else:
                k_from, v_from = (ref.at[h] for ref in splits[2 * (a - n_pair) :][:2])
            place = pl.ds(a * ROWS, ROWS)
            at = 2 * (h * n_kv + a)
            copies.append(pltpu.make_async_copy(k_from, keys.at[h, place, :], sems.at[at]))
            copies.append(pltpu.make_async_copy(v_from, values.at[h, place, :], sems.at[at + 1]))
    for h in range(HPG):
        row_copies[h].start()
        for copy in copies[2 * h * n_kv : 2 * (h + 1) * n_kv]:
            copy.start()

    def ready(head):
        row_copies[head].wait()
        for copy in copies[2 * head * n_kv : 2 * (head + 1) * n_kv]:
            copy.wait()

    attend_heads(rows, keys, values, out, ready)


def next_kernel(queries, keys, values, out, rows, row_sems):
    row_copies = query_copies(queries, rows, row_sems)
    for copy in row_copies:
        copy.start()
    attend_heads(rows, keys, values, out, lambda head: row_copies[head].wait())


def attention(queries, pairs, splits, packed):
    n_pair, n_split = len(pairs), len(splits) // 2
    n_keys = NX * NC * ROWS
    out = jax.ShapeDtypeStruct((HPG * (ROWS + STAT), HD), jnp.bfloat16)
    kv = jax.ShapeDtypeStruct((HPG, n_keys, HD), jnp.bfloat16)
    rows = pltpu.VMEM((HPG, ROWS, HD), jnp.bfloat16)
    row_sems = pltpu.SemaphoreType.DMA((HPG,))
    cost = pl.CostEstimate(
        flops=16 * HPG * ROWS * n_keys * HD,
        bytes_accessed=8 << 20,
        transcendentals=HPG * ROWS * n_keys,
    )
    if packed is None:
        return pl.pallas_call(
            functools.partial(first_kernel, n_pair, n_split),
            out_shape=(out, kv, kv),
            in_specs=[ANY] * (1 + n_pair + 2 * n_split),
            out_specs=(VMEM, VMEM, VMEM),
            scratch_shapes=[
                rows, pltpu.SemaphoreType.DMA((2 * HPG * (n_pair + n_split),)), row_sems,
            ],
            compiler_params=params(32),
            cost_estimate=cost,
        )(queries, *pairs, *splits)
    return pl.pallas_call(
        next_kernel,
        out_shape=out,
        in_specs=[ANY, VMEM, VMEM],
        out_specs=VMEM,
        scratch_shapes=[rows, row_sems],
        compiler_params=params(32),
        cost_estimate=cost,
    )(queries, *packed)


def merge_kernel(zl_ref, o0, o1, o2, o3, keep, send, merged):
    parts = (o0, o1, o2, o3)
    for h in range(HPG):
        at = h * (ROWS + STAT)
        levels = []
        for part in parts:
            tile = part[at + ROWS : at + ROWS + STAT, :].astype(jnp.float32)
            levels.append(tile[0:4, :] + tile[4:8, :] + tile[8:12, :])
        peak = functools.reduce(jnp.maximum, levels)
        shares = [jnp.exp2(level - peak) for level in levels]
        mass = functools.reduce(jnp.add, shares)
        shares = [share / mass for share in shares]
        flat = jnp.concatenate(shares + [jnp.zeros((HD - 4 * NY, HD), jnp.float32)], axis=0)
        turned = jnp.transpose(flat)
        done = 0
        for g, start in enumerate(chunk_starts()):
            total = None
            for s, part in enumerate(parts):
                share = turned[done - start : HD, 4 * s + g : 4 * s + g + 1]
                rows = part[at + done : at + start + HD, :].astype(jnp.float32)
                total = rows * share if total is None else total + rows * share
            merged[done : start + HD, h * HD : (h + 1) * HD] = total.astype(jnp.bfloat16)
            done = start + HD
    zl = zl_ref[0]
    keep[...] = merged[pl.ds(pl.multiple_of(zl * HALF, 32), HALF), :]
    send[...] = merged[pl.ds(pl.multiple_of((1 - zl) * HALF, 32), HALF), :]


def weight_loads(same, if_same, if_not, buffers, sems):
    cols = buffers.shape[3]

    def load(source, t, i):
        return pltpu.make_async_copy(
            source.at[:, pl.ds(i * cols, cols)], buffers.at[t, i], sems.at[t, i]
        )

    @pl.when(same == 1)
    def _():
        for i in range(buffers.shape[1]):
            for t in range(2):
                load(if_same[t], t, i).start()

    @pl.when(same != 1)
    def _():
        for i in range(buffers.shape[1]):
            for t in range(2):
                load(if_not[t], t, i).start()

    def ready(i):
        for t in range(2):
            load(if_same[t], t, i).wait()

    return ready


def halves(rows, weights):
    return (
        jnp.dot(rows[0:VHALF, :], weights[0], preferred_element_type=jnp.float32),
        jnp.dot(rows[VHALF:HALF, :], weights[1], preferred_element_type=jnp.float32),
    )


def project_kept_kernel(same, kept, wv_m, wv_o, wa_m, wa_o, out, buffers, sems):
    ready = weight_loads(same[0], (wv_m, wa_m), (wv_o, wa_o), buffers, sems)
    cols = buffers.shape[3]
    for i in range(buffers.shape[1]):
        ready(i)
        video, audio = halves(kept, (buffers[0, i], buffers[1, i]))
        out[0:VHALF, i * cols : (i + 1) * cols] = video
        out[VHALF:HALF, i * cols : (i + 1) * cols] = audio


def project_came_kernel(same, came, part, wv_m, wv_o, wa_m, wa_o, own, *refs):
    sides, (buffers, sems) = refs[:-2], refs[-2:]
    ready = weight_loads(same[0], (wv_o, wa_o), (wv_m, wa_m), buffers, sems)
    count, cols = buffers.shape[1], buffers.shape[3]
    for i in range(count):
        ready(i)
        at = slice(i * cols, (i + 1) * cols)
        video, audio = halves(came, (buffers[0, i], buffers[1, i]))
        video = (video + part[0:VHALF, at]).astype(jnp.bfloat16)
        audio = (audio + part[VHALF:HALF, at]).astype(jnp.bfloat16)
        upper = i // (count // 2)
        within = slice((i - upper * (count // 2)) * cols, (i + 1 - upper * (count // 2)) * cols)
        for r in range(NZH):
            target, place = (own, at) if r == 0 else (sides[2 * (r - 1) + upper], within)
            target[0:TV_L, place] = video[r * TV_L : (r + 1) * TV_L, :]
            target[TV_L:T_L, place] = audio[r * TA_L : (r + 1) * TA_L, :]


def finish_kernel(own, a_one, a_two, b_one, b_two, xv, xa, gv, ga, out_v, out_a):
    half = a_one.shape[1]
    for at, one, two in ((0, a_one, a_two), (half, b_one, b_two)):
        cols = slice(at, at + half)
        proj = (
            own[:, cols].astype(jnp.float32)
            + one[...].astype(jnp.float32)
            + two[...].astype(jnp.float32)
        )
        out_v[:, cols] = (
            xv[:, cols].astype(jnp.float32) + gv[:, cols] * proj[0:TV_L, :]
        ).astype(jnp.bfloat16)
        out_a[:, cols] = (
            xa[:, cols].astype(jnp.float32) + ga[:, cols] * proj[TV_L:T_L, :]
        ).astype(jnp.bfloat16)


def params(mib):
    return pltpu.CompilerParams(vmem_limit_bytes=mib << 20)


def shift(array, axis, step, size):
    return lax.ppermute(array, axis, [(i, (i + step) % size) for i in range(size)])


def shift_z(array, step):
    def flat(z):
        return (z % NZL) * NZH + z // NZL

    pairs = [(flat(z), flat((z + step) % NZ)) for z in range(NZ)]
    return lax.ppermute(array, ("zl", "zh"), pairs)


def frame_gate(levels, frame, gate_w):
    level = lax.dynamic_slice(levels, (frame,), (1,)).astype(jnp.float32)
    level_frac = (level + 1.0) / LEVELS
    timestep = 1000.0 * FLOW_SHIFT * level_frac / (1.0 + (FLOW_SHIFT - 1.0) * level_frac)
    half_emb = gate_w.shape[0] // 2
    frequency = jnp.exp(-math.log(10000.0) * jnp.arange(half_emb, dtype=jnp.float32) / half_emb)
    angles = timestep[:, None] * frequency[None, :]
    embedding = jnp.concatenate([jnp.cos(angles), jnp.sin(angles)], axis=1)
    return jnp.dot(
        embedding,
        gate_w.astype(jnp.float32),
        precision=lax.Precision.HIGHEST,
        preferred_element_type=jnp.float32,
    )


def local(
    video_q, video_k, video_v, audio_q, audio_k, audio_v, video_x, audio_x,
    video_out_w, audio_out_w, video_gate_w, audio_gate_w, levels, video_pos, audio_pos,
):
    width = HEADS * HD
    rank = lax.axis_index(AXES)
    frame = rank // (NX * NY * NZ * NC // video_pos.shape[0])
    frequency = 10000.0 ** (-(INDEX * np.float32(2.0)) / WIDTH_OF)
    table = jnp.asarray(
        np.concatenate(
            [
                np.stack([frequency, SIGN, SECTION]),
                np.zeros((5, HD)),
                np.arange(HD)[:, None] == PARTNER[None, :],
            ]
        ).astype(np.float32)
    )
    heads = (video_q, video_k, video_v, audio_q, audio_k, audio_v)
    piece = jax.ShapeDtypeStruct((3, HPG, T_L, HD), jnp.bfloat16)
    pieces = pl.pallas_call(
        prep_kernel,
        out_shape=(piece,) * NZ,
        in_specs=[ANY] * 9,
        out_specs=(VMEM,) * NZ,
        scratch_shapes=[
            pltpu.SMEM(video_pos.shape, jnp.int32),
            pltpu.SMEM(audio_pos.shape, jnp.int32),
            *(pltpu.VMEM(array.shape, jnp.bfloat16) for array in heads),
            pltpu.VMEM(table.shape, jnp.float32),
            pltpu.VMEM((3, HEADS, TV_L, HD), jnp.bfloat16),
            pltpu.VMEM((3, HEADS, TA_L, HD), jnp.bfloat16),
            pltpu.SemaphoreType.DMA((9,)),
        ],
        compiler_params=params(60),
    )(video_pos, audio_pos, *heads, table)
    got = list(pieces)
    for j in (4, 3, 5, 2, 6, 1, 7):
        got[j] = shift_z(pieces[j], j)
    q_mine, kv_mine = pl.pallas_call(
        arrange_kernel,
        out_shape=(
            jax.ShapeDtypeStruct((HPG, ROWS, HD), jnp.bfloat16),
            jax.ShapeDtypeStruct((2, HPG, ROWS, HD), jnp.bfloat16),
        ),
        in_specs=[ANY] * NZ,
        out_specs=(VMEM, VMEM),
        scratch_shapes=[
            pltpu.VMEM((NZ,) + piece.shape, jnp.bfloat16),
            pltpu.SemaphoreType.DMA((NZ,)),
        ],
        compiler_params=params(32),
    )(*got)
    video_gate = frame_gate(levels, frame, video_gate_w)
    audio_gate = frame_gate(levels, frame, audio_gate_w)

    kv_left = shift(kv_mine, "x", 1, NX)
    kv_right = shift(kv_mine, "x", NX - 1, NX)
    steps = (1, NY - 1, 2)
    q_far = [shift(q_mine, "y", step, NY) for step in steps]
    kv_left, kv_right, kv_held, q_far[0], q_far[1], video_gate, audio_gate = (
        lax.optimization_barrier(
            (kv_left, kv_right, kv_mine, q_far[0], q_far[1], video_gate, audio_gate)
        )
    )
    k_far = shift(kv_left[0], "x", 1, NX)
    v_far = shift(kv_right[1], "x", NX - 1, NX)
    pairs = [kv_held, kv_left, kv_right]
    pairs = pairs + [shift(kv, "c", 1, NC) for kv in pairs]
    splits = [k_far, v_far, shift(k_far, "c", 1, NC), shift(v_far, "c", 1, NC)]

    partial, keys, values = attention(q_far[0], pairs, splits, None)
    partial, video_w, audio_w = lax.optimization_barrier((partial, video_out_w, audio_out_w))
    back = [shift(partial, "y", NY - steps[0], NY)]
    wv_other = shift(video_w, "c", 1, NC)
    wa_other = shift(audio_w, "c", 1, NC)
    queries, partial = lax.optimization_barrier((q_far[1], partial))
    partial = attention(queries, (), (), (keys, values))
    back.append(shift(partial, "y", NY - steps[1], NY))
    queries, partial, back[0] = lax.optimization_barrier((q_far[2], partial, back[0]))
    partial = attention(queries, (), (), (keys, values))
    back.append(shift(partial, "y", NY - steps[2], NY))
    queries, partial, back[1] = lax.optimization_barrier((q_mine, partial, back[1]))
    back = [attention(queries, (), (), (keys, values))] + back
    zl = lax.axis_index("zl")
    c = lax.axis_index("c")
    a_shape = jax.ShapeDtypeStruct((HALF, HPG * HD), jnp.bfloat16)
    keep, send = pl.pallas_call(
        merge_kernel,
        out_shape=(a_shape, a_shape),
        in_specs=[SMEM] + [VMEM] * NY,
        out_specs=(VMEM, VMEM),
        scratch_shapes=[pltpu.VMEM((ROWS, HPG * HD), jnp.bfloat16)],
        compiler_params=params(32),
    )(jnp.full((1,), zl, jnp.int32), *back)
    came = shift(send, "zl", 1, NZL)
    same = jnp.full((1,), zl == c, jnp.int32)
    weights = (video_out_w, wv_other, audio_out_w, wa_other)
    cols = 768
    half = width // 2
    scratch = [
        pltpu.VMEM((2, width // cols, HPG * HD, cols), jnp.bfloat16),
        pltpu.SemaphoreType.DMA((2, width // cols)),
    ]
    part = pl.pallas_call(
        project_kept_kernel,
        out_shape=jax.ShapeDtypeStruct((HALF, width), jnp.float32),
        in_specs=[SMEM, VMEM] + [ANY] * 4,
        out_specs=VMEM,
        scratch_shapes=scratch,
        compiler_params=params(20),
        cost_estimate=pl.CostEstimate(
            flops=8 * HALF * HPG * HD * width, bytes_accessed=6 << 20, transcendentals=0
        ),
    )(same, keep, *weights)
    side = jax.ShapeDtypeStruct((T_L, half), jnp.bfloat16)
    own, right_a, right_b, far_a, far_b, left_a, left_b = pl.pallas_call(
        project_came_kernel,
        out_shape=(jax.ShapeDtypeStruct((T_L, width), jnp.bfloat16),) + (side,) * 6,
        in_specs=[SMEM, VMEM, VMEM] + [ANY] * 4,
        out_specs=(VMEM,) * 7,
        scratch_shapes=scratch,
        compiler_params=params(20),
    )(same, came, part, *weights)
    far_a = shift(far_a, "zh", 1, NZH)
    far_b = shift(far_b, "zh", NZH - 1, NZH)
    b_one = shift(right_b, "zh", 1, NZH)
    a_two = shift(left_a, "zh", NZH - 1, NZH)

    def add(one, two):
        return (one.astype(jnp.float32) + two.astype(jnp.float32)).astype(jnp.bfloat16)

    a_one = shift(add(right_a, far_a), "zh", 1, NZH)
    b_two = shift(add(left_b, far_b), "zh", NZH - 1, NZH)
    return tuple(
        pl.pallas_call(
            finish_kernel,
            out_shape=(
                jax.ShapeDtypeStruct(video_x.shape, jnp.bfloat16),
                jax.ShapeDtypeStruct(audio_x.shape, jnp.bfloat16),
            ),
            in_specs=[VMEM] * 9,
            out_specs=(VMEM, VMEM),
            compiler_params=params(32),
        )(own, a_one, a_two, b_one, b_two, video_x, audio_x, video_gate, audio_gate)
    )


def solution(mesh):
    fine = Mesh(mesh.devices.reshape(NX, NY, NZL, NZH, NC), AXES)
    tokens3 = P(AXES, None, None)
    tokens2 = P(AXES, None)
    weights = P(("zh", "c"), None)
    return jax.shard_map(
        local,
        mesh=fine,
        in_specs=(
            tokens3, tokens3, tokens3, tokens3, tokens3, tokens3,
            tokens2, tokens2, weights, weights, P(), P(), P(), P(), P(AXES),
        ),
        out_specs=(tokens2, tokens2),
        check_vma=False,
    )
```

```python
import functools
import math

import jax
import jax.numpy as jnp
import numpy as np
from jax import lax
from jax.experimental import pallas as pl
from jax.experimental.pallas import tpu as pltpu
from jax.sharding import Mesh
from jax.sharding import PartitionSpec as P

GRID_W = 32
GRID_SHIFT = 5
LEVELS = 1000
FLOW_SHIFT = 5.0
HEADS = 24
HD = 128
NX, NY, NZL, NZH, NC = 4, 4, 2, 4, 2
NZ = NZL * NZH
HPG = HEADS // NZ
TV_L = 48
TA_L = 8
T_L = TV_L + TA_L
ROWS = NZ * T_L
HALF = NZH * T_L
VHALF = NZH * TV_L
CHUNK = 512
STAT = 16
AXES = ("x", "y", "zl", "zh", "c")
VMEM = pl.BlockSpec(memory_space=pltpu.VMEM)
SMEM = pl.BlockSpec(memory_space=pltpu.SMEM)
HBM = pl.BlockSpec(memory_space=pltpu.HBM)
ANY = pl.BlockSpec(memory_space=pl.ANY)
NT = (((1,), (1,)), ((), ()))


def rope_lanes():
    sixth = HD // 6
    first = HD - 4 * sixth
    partner = np.zeros(HD, np.int32)
    sign = np.zeros(HD, np.float32)
    index = np.zeros(HD, np.float32)
    width_of = np.zeros(HD, np.float32)
    section = np.zeros(HD, np.int32)
    for number, (start, width) in enumerate(
        ((0, first), (first, 2 * sixth), (first + 2 * sixth, 2 * sixth))
    ):
        half = width // 2
        for k in range(half):
            low, high = start + k, start + half + k
            partner[low], partner[high] = high, low
            sign[low], sign[high] = -1.0, 1.0
            index[low] = index[high] = k
            width_of[low] = width_of[high] = width
            section[low] = section[high] = number
    return partner, sign, index, width_of, section


PARTNER, SIGN, INDEX, WIDTH_OF, SECTION = rope_lanes()


def group_of(z):
    return (z % NZH) * NZL + z // NZH


def prep_kernel(
    vpos_in, apos_in, vq_in, vk_in, vv_in, aq_in, ak_in, av_in, table_in, out,
    vpos, apos, vq, vk, vv, aq, ak, av, table, sems,
):
    copies = [
        pltpu.make_async_copy(source, target, sems.at[i])
        for i, (source, target) in enumerate(
            (
                (vpos_in, vpos), (apos_in, apos), (table_in, table), (vq_in, vq), (aq_in, aq),
                (vk_in, vk), (ak_in, ak), (vv_in, vv), (av_in, av),
            )
        )
    ]
    for copy in copies:
        copy.start()
    rank = jnp.int32(0)
    for name, size in zip(AXES, (NX, NY, NZL, NZH, NC)):
        rank = rank * size + lax.axis_index(name)
    per_frame = NX * NY * NZ * NC // vpos_in.shape[0]
    frame = lax.div(rank, jnp.int32(per_frame))
    start = lax.rem(rank, jnp.int32(per_frame)) * TV_L
    row_v = lax.broadcasted_iota(jnp.int32, (TV_L, HD), 0)
    row_a = lax.broadcasted_iota(jnp.int32, (TA_L, HD), 0)
    within = start + row_v
    high = within >> GRID_SHIFT
    wide = within & (GRID_W - 1)
    for copy in copies[0:3]:
        copy.wait()
    section_v = jnp.broadcast_to(table[2:3, :], (TV_L, HD))
    place_v = jnp.where(
        section_v == 0.0,
        vpos[frame].astype(jnp.float32),
        jnp.where(section_v == 1.0, high.astype(jnp.float32), wide.astype(jnp.float32)),
    )
    place_a = jnp.zeros((TA_L, HD), jnp.int32)
    for i in range(TA_L):
        place_a = jnp.where(row_a == i, apos[i], place_a)
    section_a = jnp.broadcast_to(table[2:3, :], (TA_L, HD))
    place_a = jnp.where(section_a == 0.0, place_a.astype(jnp.float32), 0.0)
    turns = []
    for place in (place_v, place_a):
        angles = place * table[0:1, :]
        turns.append((jnp.cos(angles), jnp.sin(angles) * table[1:2, :]))
    perm = table[8 : 8 + HD, :].astype(jnp.bfloat16)

    def turn(ref, cos_sin, gain):
        n, heads, hd = ref.shape
        cos, sin = cos_sin[0] * gain, cos_sin[1] * gain
        u = jnp.swapaxes(ref[...], 0, 1)
        other = jnp.dot(
            u.reshape(heads * n, hd), perm, preferred_element_type=jnp.float32
        ).reshape(heads, n, hd)
        return (u.astype(jnp.float32) * cos[None] + other * sin[None]).astype(jnp.bfloat16)

    scale = math.log2(math.e) / math.sqrt(HD)
    for t, (video, audio, gain) in enumerate(((vq, aq, scale), (vk, ak, 1.0), (vv, av, None))):
        for copy in copies[3 + 2 * t : 5 + 2 * t]:
            copy.wait()
        if gain is None:
            video, audio = jnp.swapaxes(video[...], 0, 1), jnp.swapaxes(audio[...], 0, 1)
        else:
            video, audio = turn(video, turns[0], gain), turn(audio, turns[1], gain)
        for z in range(NZ):
            for h in range(HPG):
                out[z, t, h, 0:TV_L, :] = video[group_of(z) * HPG + h]
                out[z, t, h, TV_L:T_L, :] = audio[group_of(z) * HPG + h]


def arrange_kernel(got, q_out, kv_out):
    here = lax.axis_index("zh")
    for zl in range(NZL):
        for r in range(NZH):
            z = zl * NZH + lax.rem(here + r, NZH)
            v_at = zl * HALF + r * TV_L
            a_at = zl * HALF + VHALF + r * TA_L
            for h in range(HPG):
                q_out[h, v_at : v_at + TV_L, :] = got[z, 0, h, 0:TV_L, :]
                q_out[h, a_at : a_at + TA_L, :] = got[z, 0, h, TV_L:T_L, :]
                for t in range(2):
                    kv_out[t, h, v_at : v_at + TV_L, :] = got[z, 1 + t, h, 0:TV_L, :]
                    kv_out[t, h, a_at : a_at + TA_L, :] = got[z, 1 + t, h, TV_L:T_L, :]


def chunk_starts():
    return [min(at, ROWS - HD) for at in range(0, ROWS, HD)]


def stat_tile(level):
    row = lax.broadcasted_iota(jnp.int32, (STAT, HD), 0)
    flat = jnp.zeros((STAT, HD), jnp.float32)
    for g, at in enumerate(chunk_starts()):
        line = jnp.transpose(level[at : at + HD, :])[0:1, :]
        flat = jnp.where((row & 3) == g, line, flat)
    high = flat.astype(jnp.bfloat16).astype(jnp.float32)
    middle = (flat - high).astype(jnp.bfloat16).astype(jnp.float32)
    low = flat - high - middle
    tile = jnp.where(row < 4, high, jnp.where(row < 8, middle, jnp.where(row < 12, low, 0.0)))
    return tile.astype(jnp.bfloat16)


def attend_heads(queries, keys, values, out, ready):
    n_keys = keys.shape[1]
    cuts = [(at, min(CHUNK, n_keys - at)) for at in range(0, n_keys, CHUNK)]
    for head in range(HPG):
        ready(head)
        rows = queries[head]

        def scores(cut):
            at, size = cut
            return lax.dot_general(
                rows, keys[head, at : at + size, :], NT, preferred_element_type=jnp.float32
            )

        s = scores(cuts[0])
        peak = total = None
        for number, (at, size) in enumerate(cuts):
            coming = scores(cuts[number + 1]) if number + 1 < len(cuts) else None
            slabs = [s[:, g : g + HD] for g in range(0, size, HD)]
            top = jnp.max(functools.reduce(jnp.maximum, slabs), axis=1, keepdims=True)
            top = jnp.broadcast_to(top, (ROWS, HD))
            if peak is not None:
                top = jnp.maximum(peak, top)
            weights = jnp.concatenate(
                [jnp.exp2(slab - top).astype(jnp.bfloat16) for slab in slabs], axis=1
            )
            ones = jnp.ones((size, HD), jnp.bfloat16)
            new = jnp.dot(
                weights,
                jnp.concatenate([values[head, at : at + size, :], ones], axis=1),
                preferred_element_type=jnp.float32,
            )
            if total is None:
                total = new
            else:
                factor = jnp.exp2(peak - top)
                total = total * jnp.concatenate([factor, factor], axis=1) + new
            peak, s = top, coming
        mass = total[:, HD : 2 * HD]
        at = head * (ROWS + STAT)
        out[at : at + ROWS, :] = (total[:, 0:HD] / mass).astype(jnp.bfloat16)
        out[at + ROWS : at + ROWS + STAT, :] = stat_tile(peak + jnp.log2(mass))


def first_kernel(n_pair, n_split, *refs):
    queries = refs[0]
    pairs, splits = refs[1 : 1 + n_pair], refs[1 + n_pair : 1 + n_pair + 2 * n_split]
    out, keys, values, sems = refs[1 + n_pair + 2 * n_split :]
    n_kv = n_pair + n_split
    copies = []
    for h in range(HPG):
        for a in range(n_kv):
            if a < n_pair:
                k_from, v_from = pairs[a].at[0, h], pairs[a].at[1, h]
            else:
                k_from, v_from = (ref.at[h] for ref in splits[2 * (a - n_pair) :][:2])
            place = pl.ds(a * ROWS, ROWS)
            at = 2 * (h * n_kv + a)
            copies.append(pltpu.make_async_copy(k_from, keys.at[h, place, :], sems.at[at]))
            copies.append(pltpu.make_async_copy(v_from, values.at[h, place, :], sems.at[at + 1]))
    for copy in copies:
        copy.start()

    def ready(head):
        for copy in copies[2 * head * n_kv : 2 * (head + 1) * n_kv]:
            copy.wait()

    attend_heads(queries, keys, values, out, ready)


def next_kernel(queries, keys, values, out):
    attend_heads(queries, keys, values, out, lambda head: None)


def attention(queries, pairs, splits, packed):
    n_pair, n_split = len(pairs), len(splits) // 2
    n_keys = NX * NC * ROWS
    out = jax.ShapeDtypeStruct((HPG * (ROWS + STAT), HD), jnp.bfloat16)
    kv = jax.ShapeDtypeStruct((HPG, n_keys, HD), jnp.bfloat16)
    cost = pl.CostEstimate(
        flops=16 * HPG * ROWS * n_keys * HD,
        bytes_accessed=8 << 20,
        transcendentals=HPG * ROWS * n_keys,
    )
    if packed is None:
        return pl.pallas_call(
            functools.partial(first_kernel, n_pair, n_split),
            out_shape=(out, kv, kv),
            in_specs=[VMEM] + [ANY] * (n_pair + 2 * n_split),
            out_specs=(VMEM, VMEM, VMEM),
            scratch_shapes=[pltpu.SemaphoreType.DMA((2 * HPG * (n_pair + n_split),))],
            compiler_params=params(32),
            cost_estimate=cost,
        )(queries, *pairs, *splits)
    return pl.pallas_call(
        next_kernel,
        out_shape=out,
        in_specs=[VMEM] * 3,
        out_specs=VMEM,
        compiler_params=params(32),
        cost_estimate=cost,
    )(queries, *packed)


def merge_kernel(zl_ref, o0, o1, o2, o3, keep, send, merged):
    parts = (o0, o1, o2, o3)
    for h in range(HPG):
        at = h * (ROWS + STAT)
        levels = []
        for part in parts:
            tile = part[at + ROWS : at + ROWS + STAT, :].astype(jnp.float32)
            levels.append(tile[0:4, :] + tile[4:8, :] + tile[8:12, :])
        peak = functools.reduce(jnp.maximum, levels)
        shares = [jnp.exp2(level - peak) for level in levels]
        mass = functools.reduce(jnp.add, shares)
        shares = [share / mass for share in shares]
        flat = jnp.concatenate(shares + [jnp.zeros((HD - 4 * NY, HD), jnp.float32)], axis=0)
        turned = jnp.transpose(flat)
        done = 0
        for g, start in enumerate(chunk_starts()):
            total = None
            for s, part in enumerate(parts):
                share = turned[done - start : HD, 4 * s + g : 4 * s + g + 1]
                rows = part[at + done : at + start + HD, :].astype(jnp.float32)
                total = rows * share if total is None else total + rows * share
            merged[done : start + HD, h * HD : (h + 1) * HD] = total.astype(jnp.bfloat16)
            done = start + HD
    zl = zl_ref[0]
    keep[...] = merged[pl.ds(pl.multiple_of(zl * HALF, 32), HALF), :]
    send[...] = merged[pl.ds(pl.multiple_of((1 - zl) * HALF, 32), HALF), :]


def weight_loads(same, if_same, if_not, buffers, sems):
    cols = buffers.shape[3]

    def load(source, t, i):
        return pltpu.make_async_copy(
            source.at[:, pl.ds(i * cols, cols)], buffers.at[t, i], sems.at[t, i]
        )

    @pl.when(same == 1)
    def _():
        for i in range(buffers.shape[1]):
            for t in range(2):
                load(if_same[t], t, i).start()

    @pl.when(same != 1)
    def _():
        for i in range(buffers.shape[1]):
            for t in range(2):
                load(if_not[t], t, i).start()

    def ready(i):
        for t in range(2):
            load(if_same[t], t, i).wait()

    return ready


def halves(rows, weights):
    return (
        jnp.dot(rows[0:VHALF, :], weights[0], preferred_element_type=jnp.float32),
        jnp.dot(rows[VHALF:HALF, :], weights[1], preferred_element_type=jnp.float32),
    )


def project_kept_kernel(same, kept, wv_m, wv_o, wa_m, wa_o, out, buffers, sems):
    ready = weight_loads(same[0], (wv_m, wa_m), (wv_o, wa_o), buffers, sems)
    cols = buffers.shape[3]
    for i in range(buffers.shape[1]):
        ready(i)
        video, audio = halves(kept, (buffers[0, i], buffers[1, i]))
        out[0:VHALF, i * cols : (i + 1) * cols] = video
        out[VHALF:HALF, i * cols : (i + 1) * cols] = audio


def project_came_kernel(same, came, part, wv_m, wv_o, wa_m, wa_o, own, *refs):
    sides, (buffers, sems) = refs[:-2], refs[-2:]
    ready = weight_loads(same[0], (wv_o, wa_o), (wv_m, wa_m), buffers, sems)
    count, cols = buffers.shape[1], buffers.shape[3]
    for i in range(count):
        ready(i)
        at = slice(i * cols, (i + 1) * cols)
        video, audio = halves(came, (buffers[0, i], buffers[1, i]))
        video = (video + part[0:VHALF, at]).astype(jnp.bfloat16)
        audio = (audio + part[VHALF:HALF, at]).astype(jnp.bfloat16)
        upper = i // (count // 2)
        within = slice((i - upper * (count // 2)) * cols, (i + 1 - upper * (count // 2)) * cols)
        for r in range(NZH):
            target, place = (own, at) if r == 0 else (sides[2 * (r - 1) + upper], within)
            target[0:TV_L, place] = video[r * TV_L : (r + 1) * TV_L, :]
            target[TV_L:T_L, place] = audio[r * TA_L : (r + 1) * TA_L, :]


def finish_kernel(own, a_one, a_two, b_one, b_two, xv, xa, gv, ga, out_v, out_a):
    half = a_one.shape[1]
    for at, one, two in ((0, a_one, a_two), (half, b_one, b_two)):
        cols = slice(at, at + half)
        proj = (
            own[:, cols].astype(jnp.float32)
            + one[...].astype(jnp.float32)
            + two[...].astype(jnp.float32)
        )
        out_v[:, cols] = (
            xv[:, cols].astype(jnp.float32) + gv[:, cols] * proj[0:TV_L, :]
        ).astype(jnp.bfloat16)
        out_a[:, cols] = (
            xa[:, cols].astype(jnp.float32) + ga[:, cols] * proj[TV_L:T_L, :]
        ).astype(jnp.bfloat16)


def params(mib):
    return pltpu.CompilerParams(vmem_limit_bytes=mib << 20)


def shift(array, axis, step, size):
    return lax.ppermute(array, axis, [(i, (i + step) % size) for i in range(size)])


def frame_gate(levels, frame, gate_w):
    level = lax.dynamic_slice(levels, (frame,), (1,)).astype(jnp.float32)
    level_frac = (level + 1.0) / LEVELS
    timestep = 1000.0 * FLOW_SHIFT * level_frac / (1.0 + (FLOW_SHIFT - 1.0) * level_frac)
    half_emb = gate_w.shape[0] // 2
    frequency = jnp.exp(-math.log(10000.0) * jnp.arange(half_emb, dtype=jnp.float32) / half_emb)
    angles = timestep[:, None] * frequency[None, :]
    embedding = jnp.concatenate([jnp.cos(angles), jnp.sin(angles)], axis=1)
    return jnp.dot(
        embedding,
        gate_w.astype(jnp.float32),
        precision=lax.Precision.HIGHEST,
        preferred_element_type=jnp.float32,
    )


def local(
    video_q, video_k, video_v, audio_q, audio_k, audio_v, video_x, audio_x,
    video_out_w, audio_out_w, video_gate_w, audio_gate_w, levels, video_pos, audio_pos,
):
    width = HEADS * HD
    rank = lax.axis_index(AXES)
    frame = rank // (NX * NY * NZ * NC // video_pos.shape[0])
    frequency = 10000.0 ** (-(INDEX * np.float32(2.0)) / WIDTH_OF)
    table = jnp.asarray(
        np.concatenate(
            [
                np.stack([frequency, SIGN, SECTION]),
                np.zeros((5, HD)),
                np.arange(HD)[:, None] == PARTNER[None, :],
            ]
        ).astype(np.float32)
    )
    heads = (video_q, video_k, video_v, audio_q, audio_k, audio_v)
    packed = pl.pallas_call(
        prep_kernel,
        out_shape=jax.ShapeDtypeStruct((NZ, 3, HPG, T_L, HD), jnp.bfloat16),
        in_specs=[ANY] * 9,
        out_specs=VMEM,
        scratch_shapes=[
            pltpu.SMEM(video_pos.shape, jnp.int32),
            pltpu.SMEM(audio_pos.shape, jnp.int32),
            *(pltpu.VMEM(array.shape, jnp.bfloat16) for array in heads),
            pltpu.VMEM(table.shape, jnp.float32),
            pltpu.SemaphoreType.DMA((9,)),
        ],
        compiler_params=params(60),
    )(video_pos, audio_pos, *heads, table)
    got = lax.all_to_all(packed, ("zl", "zh"), split_axis=0, concat_axis=0, tiled=True)
    q_mine, kv_mine = pl.pallas_call(
        arrange_kernel,
        out_shape=(
            jax.ShapeDtypeStruct((HPG, ROWS, HD), jnp.bfloat16),
            jax.ShapeDtypeStruct((2, HPG, ROWS, HD), jnp.bfloat16),
        ),
        in_specs=[VMEM],
        out_specs=(VMEM, VMEM),
        compiler_params=params(32),
    )(got)

    video_gate = frame_gate(levels, frame, video_gate_w)
    audio_gate = frame_gate(levels, frame, audio_gate_w)
    kv_left = shift(kv_mine, "x", 1, NX)
    kv_right = shift(kv_mine, "x", NX - 1, NX)
    steps = (1, NY - 1, 2)
    q_far = [shift(q_mine, "y", step, NY) for step in steps]
    kv_left, kv_right, kv_held, q_far[0], q_far[1], video_gate, audio_gate = (
        lax.optimization_barrier(
            (kv_left, kv_right, kv_mine, q_far[0], q_far[1], video_gate, audio_gate)
        )
    )
    k_far = shift(kv_left[0], "x", 1, NX)
    v_far = shift(kv_right[1], "x", NX - 1, NX)
    pairs = [kv_held, kv_left, kv_right]
    pairs = pairs + [shift(kv, "c", 1, NC) for kv in pairs]
    splits = [k_far, v_far, shift(k_far, "c", 1, NC), shift(v_far, "c", 1, NC)]

    partial, keys, values = attention(q_far[0], pairs, splits, None)
    video_w, audio_w = video_out_w, audio_out_w
    back = [shift(partial, "y", NY - steps[0], NY)]
    wv_other = shift(video_w, "c", 1, NC)
    wa_other = shift(audio_w, "c", 1, NC)
    queries, partial = lax.optimization_barrier((q_far[1], partial))
    partial = attention(queries, (), (), (keys, values))
    back.append(shift(partial, "y", NY - steps[1], NY))
    queries, partial, back[0] = lax.optimization_barrier((q_far[2], partial, back[0]))
    partial = attention(queries, (), (), (keys, values))
    back.append(shift(partial, "y", NY - steps[2], NY))
    queries, partial, back[1] = lax.optimization_barrier((q_mine, partial, back[1]))
    back = [attention(queries, (), (), (keys, values))] + back
    zl = lax.axis_index("zl")
    c = lax.axis_index("c")
    a_shape = jax.ShapeDtypeStruct((HALF, HPG * HD), jnp.bfloat16)
    keep, send = pl.pallas_call(
        merge_kernel,
        out_shape=(a_shape, a_shape),
        in_specs=[SMEM] + [VMEM] * NY,
        out_specs=(VMEM, VMEM),
        scratch_shapes=[pltpu.VMEM((ROWS, HPG * HD), jnp.bfloat16)],
        compiler_params=params(32),
    )(jnp.full((1,), zl, jnp.int32), *back)
    came = shift(send, "zl", 1, NZL)
    same = jnp.full((1,), zl == c, jnp.int32)
    weights = (video_out_w, wv_other, audio_out_w, wa_other)
    cols = 768
    half = width // 2
    scratch = [
        pltpu.VMEM((2, width // cols, HPG * HD, cols), jnp.bfloat16),
        pltpu.SemaphoreType.DMA((2, width // cols)),
    ]
    part = pl.pallas_call(
        project_kept_kernel,
        out_shape=jax.ShapeDtypeStruct((HALF, width), jnp.float32),
        in_specs=[SMEM, VMEM] + [HBM] * 4,
        out_specs=VMEM,
        scratch_shapes=scratch,
        compiler_params=params(20),
        cost_estimate=pl.CostEstimate(
            flops=8 * HALF * HPG * HD * width, bytes_accessed=6 << 20, transcendentals=0
        ),
    )(same, keep, *weights)
    side = jax.ShapeDtypeStruct((T_L, half), jnp.bfloat16)
    own, right_a, right_b, far_a, far_b, left_a, left_b = pl.pallas_call(
        project_came_kernel,
        out_shape=(jax.ShapeDtypeStruct((T_L, width), jnp.bfloat16),) + (side,) * 6,
        in_specs=[SMEM, VMEM, VMEM] + [HBM] * 4,
        out_specs=(VMEM,) * 7,
        scratch_shapes=scratch,
        compiler_params=params(20),
    )(same, came, part, *weights)
    far_a = shift(far_a, "zh", 1, NZH)
    far_b = shift(far_b, "zh", NZH - 1, NZH)
    b_one = shift(right_b, "zh", 1, NZH)
    a_two = shift(left_a, "zh", NZH - 1, NZH)

    def add(one, two):
        return (one.astype(jnp.float32) + two.astype(jnp.float32)).astype(jnp.bfloat16)

    a_one = shift(add(right_a, far_a), "zh", 1, NZH)
    b_two = shift(add(left_b, far_b), "zh", NZH - 1, NZH)
    return tuple(
        pl.pallas_call(
            finish_kernel,
            out_shape=(
                jax.ShapeDtypeStruct(video_x.shape, jnp.bfloat16),
                jax.ShapeDtypeStruct(audio_x.shape, jnp.bfloat16),
            ),
            in_specs=[VMEM] * 9,
            out_specs=(VMEM, VMEM),
            compiler_params=params(32),
        )(own, a_one, a_two, b_one, b_two, video_x, audio_x, video_gate, audio_gate)
    )


def solution(mesh):
    fine = Mesh(mesh.devices.reshape(NX, NY, NZL, NZH, NC), AXES)
    tokens3 = P(AXES, None, None)
    tokens2 = P(AXES, None)
    weights = P(("zh", "c"), None)
    return jax.shard_map(
        local,
        mesh=fine,
        in_specs=(
            tokens3, tokens3, tokens3, tokens3, tokens3, tokens3,
            tokens2, tokens2, weights, weights, P(), P(), P(), P(), P(AXES),
        ),
        out_specs=(tokens2, tokens2),
        check_vma=False,
    )
```

```python
import functools
import math

import jax
import jax.numpy as jnp
import numpy as np
from jax import lax
from jax.experimental import pallas as pl
from jax.experimental.pallas import tpu as pltpu
from jax.sharding import Mesh
from jax.sharding import PartitionSpec as P

GRID_W = 32
GRID_SHIFT = 5
LEVELS = 1000
FLOW_SHIFT = 5.0
HEADS = 24
HD = 128
NX, NY, NZL, NZH, NC = 4, 4, 2, 4, 2
NZ = NZL * NZH
HPG = HEADS // NZ
TV_L = 48
TA_L = 8
T_L = TV_L + TA_L
ROWS = NZ * T_L
HALF = NZH * T_L
VHALF = NZH * TV_L
CHUNK = 512
STAT = 16
AXES = ("x", "y", "zl", "zh", "c")
VMEM = pl.BlockSpec(memory_space=pltpu.VMEM)
SMEM = pl.BlockSpec(memory_space=pltpu.SMEM)
HBM = pl.BlockSpec(memory_space=pltpu.HBM)
ANY = pl.BlockSpec(memory_space=pl.ANY)
NT = (((1,), (1,)), ((), ()))


def rope_lanes():
    sixth = HD // 6
    first = HD - 4 * sixth
    partner = np.zeros(HD, np.int32)
    sign = np.zeros(HD, np.float32)
    index = np.zeros(HD, np.float32)
    width_of = np.zeros(HD, np.float32)
    section = np.zeros(HD, np.int32)
    for number, (start, width) in enumerate(
        ((0, first), (first, 2 * sixth), (first + 2 * sixth, 2 * sixth))
    ):
        half = width // 2
        for k in range(half):
            low, high = start + k, start + half + k
            partner[low], partner[high] = high, low
            sign[low], sign[high] = -1.0, 1.0
            index[low] = index[high] = k
            width_of[low] = width_of[high] = width
            section[low] = section[high] = number
    return partner, sign, index, width_of, section


PARTNER, SIGN, INDEX, WIDTH_OF, SECTION = rope_lanes()


def group_of(z):
    return (z % NZH) * NZL + z // NZH


def prep_kernel(
    vpos_in, apos_in, vq_in, vk_in, vv_in, aq_in, ak_in, av_in, table_in, out,
    vpos, apos, vq, vk, vv, aq, ak, av, table, sems,
):
    copies = [
        pltpu.make_async_copy(source, target, sems.at[i])
        for i, (source, target) in enumerate(
            (
                (vpos_in, vpos), (apos_in, apos), (table_in, table), (vq_in, vq), (aq_in, aq),
                (vk_in, vk), (ak_in, ak), (vv_in, vv), (av_in, av),
            )
        )
    ]
    for copy in copies:
        copy.start()
    rank = jnp.int32(0)
    for name, size in zip(AXES, (NX, NY, NZL, NZH, NC)):
        rank = rank * size + lax.axis_index(name)
    per_frame = NX * NY * NZ * NC // vpos_in.shape[0]
    frame = lax.div(rank, jnp.int32(per_frame))
    start = lax.rem(rank, jnp.int32(per_frame)) * TV_L
    row_v = lax.broadcasted_iota(jnp.int32, (TV_L, HD), 0)
    row_a = lax.broadcasted_iota(jnp.int32, (TA_L, HD), 0)
    within = start + row_v
    high = within >> GRID_SHIFT
    wide = within & (GRID_W - 1)
    for copy in copies[0:3]:
        copy.wait()
    section_v = jnp.broadcast_to(table[2:3, :], (TV_L, HD))
    place_v = jnp.where(
        section_v == 0.0,
        vpos[frame].astype(jnp.float32),
        jnp.where(section_v == 1.0, high.astype(jnp.float32), wide.astype(jnp.float32)),
    )
    place_a = jnp.zeros((TA_L, HD), jnp.int32)
    for i in range(TA_L):
        place_a = jnp.where(row_a == i, apos[i], place_a)
    section_a = jnp.broadcast_to(table[2:3, :], (TA_L, HD))
    place_a = jnp.where(section_a == 0.0, place_a.astype(jnp.float32), 0.0)
    turns = []
    for place in (place_v, place_a):
        angles = place * table[0:1, :]
        turns.append((jnp.cos(angles), jnp.sin(angles) * table[1:2, :]))
    perm = table[8 : 8 + HD, :].astype(jnp.bfloat16)

    def turn(ref, cos_sin, gain):
        n, heads, hd = ref.shape
        cos, sin = cos_sin[0] * gain, cos_sin[1] * gain
        u = jnp.swapaxes(ref[...], 0, 1)
        other = jnp.dot(
            u.reshape(heads * n, hd), perm, preferred_element_type=jnp.float32
        ).reshape(heads, n, hd)
        return (u.astype(jnp.float32) * cos[None] + other * sin[None]).astype(jnp.bfloat16)

    scale = math.log2(math.e) / math.sqrt(HD)
    for t, (video, audio, gain) in enumerate(((vq, aq, scale), (vk, ak, 1.0), (vv, av, None))):
        for copy in copies[3 + 2 * t : 5 + 2 * t]:
            copy.wait()
        if gain is None:
            video, audio = jnp.swapaxes(video[...], 0, 1), jnp.swapaxes(audio[...], 0, 1)
        else:
            video, audio = turn(video, turns[0], gain), turn(audio, turns[1], gain)
        for z in range(NZ):
            for h in range(HPG):
                out[z, t, h, 0:TV_L, :] = video[group_of(z) * HPG + h]
                out[z, t, h, TV_L:T_L, :] = audio[group_of(z) * HPG + h]


def arrange_kernel(got, q_out, kv_out):
    here = lax.axis_index("zh")
    for zl in range(NZL):
        for r in range(NZH):
            z = zl * NZH + lax.rem(here + r, NZH)
            v_at = zl * HALF + r * TV_L
            a_at = zl * HALF + VHALF + r * TA_L
            for h in range(HPG):
                q_out[h, v_at : v_at + TV_L, :] = got[z, 0, h, 0:TV_L, :]
                q_out[h, a_at : a_at + TA_L, :] = got[z, 0, h, TV_L:T_L, :]
                for t in range(2):
                    kv_out[t, h, v_at : v_at + TV_L, :] = got[z, 1 + t, h, 0:TV_L, :]
                    kv_out[t, h, a_at : a_at + TA_L, :] = got[z, 1 + t, h, TV_L:T_L, :]


def chunk_starts():
    return [min(at, ROWS - HD) for at in range(0, ROWS, HD)]


def stat_tile(level):
    row = lax.broadcasted_iota(jnp.int32, (STAT, HD), 0)
    flat = jnp.zeros((STAT, HD), jnp.float32)
    for g, at in enumerate(chunk_starts()):
        line = jnp.transpose(level[at : at + HD, :])[0:1, :]
        flat = jnp.where((row & 3) == g, line, flat)
    high = flat.astype(jnp.bfloat16).astype(jnp.float32)
    middle = (flat - high).astype(jnp.bfloat16).astype(jnp.float32)
    low = flat - high - middle
    tile = jnp.where(row < 4, high, jnp.where(row < 8, middle, jnp.where(row < 12, low, 0.0)))
    return tile.astype(jnp.bfloat16)


def attend_heads(queries, keys, values, out, ready):
    n_keys = keys.shape[1]
    cuts = [(at, min(CHUNK, n_keys - at)) for at in range(0, n_keys, CHUNK)]
    for head in range(HPG):
        ready(head)
        rows = queries[head]

        def scores(cut):
            at, size = cut
            return lax.dot_general(
                rows, keys[head, at : at + size, :], NT, preferred_element_type=jnp.float32
            )

        s = scores(cuts[0])
        peak = total = None
        for number, (at, size) in enumerate(cuts):
            coming = scores(cuts[number + 1]) if number + 1 < len(cuts) else None
            slabs = [s[:, g : g + HD] for g in range(0, size, HD)]
            top = jnp.max(functools.reduce(jnp.maximum, slabs), axis=1, keepdims=True)
            top = jnp.broadcast_to(top, (ROWS, HD))
            if peak is not None:
                top = jnp.maximum(peak, top)
            weights = jnp.concatenate(
                [jnp.exp2(slab - top).astype(jnp.bfloat16) for slab in slabs], axis=1
            )
            ones = jnp.ones((size, HD), jnp.bfloat16)
            new = jnp.dot(
                weights,
                jnp.concatenate([values[head, at : at + size, :], ones], axis=1),
                preferred_element_type=jnp.float32,
            )
            if total is None:
                total = new
            else:
                factor = jnp.exp2(peak - top)
                total = total * jnp.concatenate([factor, factor], axis=1) + new
            peak, s = top, coming
        mass = total[:, HD : 2 * HD]
        at = head * (ROWS + STAT)
        out[at : at + ROWS, :] = (total[:, 0:HD] / mass).astype(jnp.bfloat16)
        out[at + ROWS : at + ROWS + STAT, :] = stat_tile(peak + jnp.log2(mass))


def first_kernel(n_pair, n_split, *refs):
    queries = refs[0]
    pairs, splits = refs[1 : 1 + n_pair], refs[1 + n_pair : 1 + n_pair + 2 * n_split]
    out, keys, values, sems = refs[1 + n_pair + 2 * n_split :]
    n_kv = n_pair + n_split
    copies = []
    for h in range(HPG):
        for a in range(n_kv):
            if a < n_pair:
                k_from, v_from = pairs[a].at[0, h], pairs[a].at[1, h]
            else:
                k_from, v_from = (ref.at[h] for ref in splits[2 * (a - n_pair) :][:2])
            place = pl.ds(a * ROWS, ROWS)
            at = 2 * (h * n_kv + a)
            copies.append(pltpu.make_async_copy(k_from, keys.at[h, place, :], sems.at[at]))
            copies.append(pltpu.make_async_copy(v_from, values.at[h, place, :], sems.at[at + 1]))
    for copy in copies:
        copy.start()

    def ready(head):
        for copy in copies[2 * head * n_kv : 2 * (head + 1) * n_kv]:
            copy.wait()

    attend_heads(queries, keys, values, out, ready)


def next_kernel(queries, keys, values, out):
    attend_heads(queries, keys, values, out, lambda head: None)


def attention(queries, pairs, splits, packed):
    n_pair, n_split = len(pairs), len(splits) // 2
    n_keys = NX * NC * ROWS
    out = jax.ShapeDtypeStruct((HPG * (ROWS + STAT), HD), jnp.bfloat16)
    kv = jax.ShapeDtypeStruct((HPG, n_keys, HD), jnp.bfloat16)
    cost = pl.CostEstimate(
        flops=16 * HPG * ROWS * n_keys * HD,
        bytes_accessed=8 << 20,
        transcendentals=HPG * ROWS * n_keys,
    )
    if packed is None:
        return pl.pallas_call(
            functools.partial(first_kernel, n_pair, n_split),
            out_shape=(out, kv, kv),
            in_specs=[VMEM] + [ANY] * (n_pair + 2 * n_split),
            out_specs=(VMEM, VMEM, VMEM),
            scratch_shapes=[pltpu.SemaphoreType.DMA((2 * HPG * (n_pair + n_split),))],
            compiler_params=params(32),
            cost_estimate=cost,
        )(queries, *pairs, *splits)
    return pl.pallas_call(
        next_kernel,
        out_shape=out,
        in_specs=[VMEM] * 3,
        out_specs=VMEM,
        compiler_params=params(32),
        cost_estimate=cost,
    )(queries, *packed)


def merge_kernel(zl_ref, o0, o1, o2, o3, keep, send, merged):
    parts = (o0, o1, o2, o3)
    for h in range(HPG):
        at = h * (ROWS + STAT)
        levels = []
        for part in parts:
            tile = part[at + ROWS : at + ROWS + STAT, :].astype(jnp.float32)
            levels.append(tile[0:4, :] + tile[4:8, :] + tile[8:12, :])
        peak = functools.reduce(jnp.maximum, levels)
        shares = [jnp.exp2(level - peak) for level in levels]
        mass = functools.reduce(jnp.add, shares)
        shares = [share / mass for share in shares]
        flat = jnp.concatenate(shares + [jnp.zeros((HD - 4 * NY, HD), jnp.float32)], axis=0)
        turned = jnp.transpose(flat)
        done = 0
        for g, start in enumerate(chunk_starts()):
            total = None
            for s, part in enumerate(parts):
                share = turned[done - start : HD, 4 * s + g : 4 * s + g + 1]
                rows = part[at + done : at + start + HD, :].astype(jnp.float32)
                total = rows * share if total is None else total + rows * share
            merged[done : start + HD, h * HD : (h + 1) * HD] = total.astype(jnp.bfloat16)
            done = start + HD
    zl = zl_ref[0]
    keep[...] = merged[pl.ds(pl.multiple_of(zl * HALF, 32), HALF), :]
    send[...] = merged[pl.ds(pl.multiple_of((1 - zl) * HALF, 32), HALF), :]


def weight_loads(same, if_same, if_not, buffers, sems):
    cols = buffers.shape[3]

    def load(source, t, i):
        return pltpu.make_async_copy(
            source.at[:, pl.ds(i * cols, cols)], buffers.at[t, i], sems.at[t, i]
        )

    @pl.when(same == 1)
    def _():
        for i in range(buffers.shape[1]):
            for t in range(2):
                load(if_same[t], t, i).start()

    @pl.when(same != 1)
    def _():
        for i in range(buffers.shape[1]):
            for t in range(2):
                load(if_not[t], t, i).start()

    def ready(i):
        for t in range(2):
            load(if_same[t], t, i).wait()

    return ready


def halves(rows, weights):
    return (
        jnp.dot(rows[0:VHALF, :], weights[0], preferred_element_type=jnp.float32),
        jnp.dot(rows[VHALF:HALF, :], weights[1], preferred_element_type=jnp.float32),
    )


def project_kept_kernel(same, kept, wv_m, wv_o, wa_m, wa_o, out, buffers, sems):
    ready = weight_loads(same[0], (wv_m, wa_m), (wv_o, wa_o), buffers, sems)
    cols = buffers.shape[3]
    for i in range(buffers.shape[1]):
        ready(i)
        video, audio = halves(kept, (buffers[0, i], buffers[1, i]))
        out[0:VHALF, i * cols : (i + 1) * cols] = video
        out[VHALF:HALF, i * cols : (i + 1) * cols] = audio


def project_came_kernel(same, came, part, wv_m, wv_o, wa_m, wa_o, own, *refs):
    sides, (buffers, sems) = refs[:-2], refs[-2:]
    ready = weight_loads(same[0], (wv_o, wa_o), (wv_m, wa_m), buffers, sems)
    count, cols = buffers.shape[1], buffers.shape[3]
    for i in range(count):
        ready(i)
        at = slice(i * cols, (i + 1) * cols)
        video, audio = halves(came, (buffers[0, i], buffers[1, i]))
        video = (video + part[0:VHALF, at]).astype(jnp.bfloat16)
        audio = (audio + part[VHALF:HALF, at]).astype(jnp.bfloat16)
        upper = i // (count // 2)
        within = slice((i - upper * (count // 2)) * cols, (i + 1 - upper * (count // 2)) * cols)
        for r in range(NZH):
            target, place = (own, at) if r == 0 else (sides[2 * (r - 1) + upper], within)
            target[0:TV_L, place] = video[r * TV_L : (r + 1) * TV_L, :]
            target[TV_L:T_L, place] = audio[r * TA_L : (r + 1) * TA_L, :]


def finish_kernel(own, a_one, a_two, b_one, b_two, xv, xa, gv, ga, out_v, out_a):
    half = a_one.shape[1]
    for at, one, two in ((0, a_one, a_two), (half, b_one, b_two)):
        cols = slice(at, at + half)
        proj = (
            own[:, cols].astype(jnp.float32)
            + one[...].astype(jnp.float32)
            + two[...].astype(jnp.float32)
        )
        out_v[:, cols] = (
            xv[:, cols].astype(jnp.float32) + gv[:, cols] * proj[0:TV_L, :]
        ).astype(jnp.bfloat16)
        out_a[:, cols] = (
            xa[:, cols].astype(jnp.float32) + ga[:, cols] * proj[TV_L:T_L, :]
        ).astype(jnp.bfloat16)


def params(mib):
    return pltpu.CompilerParams(vmem_limit_bytes=mib << 20)


def shift(array, axis, step, size):
    return lax.ppermute(array, axis, [(i, (i + step) % size) for i in range(size)])


def frame_gate(levels, frame, gate_w):
    level = lax.dynamic_slice(levels, (frame,), (1,)).astype(jnp.float32)
    level_frac = (level + 1.0) / LEVELS
    timestep = 1000.0 * FLOW_SHIFT * level_frac / (1.0 + (FLOW_SHIFT - 1.0) * level_frac)
    half_emb = gate_w.shape[0] // 2
    frequency = jnp.exp(-math.log(10000.0) * jnp.arange(half_emb, dtype=jnp.float32) / half_emb)
    angles = timestep[:, None] * frequency[None, :]
    embedding = jnp.concatenate([jnp.cos(angles), jnp.sin(angles)], axis=1)
    return jnp.dot(
        embedding,
        gate_w.astype(jnp.float32),
        precision=lax.Precision.HIGHEST,
        preferred_element_type=jnp.float32,
    )


def local(
    video_q, video_k, video_v, audio_q, audio_k, audio_v, video_x, audio_x,
    video_out_w, audio_out_w, video_gate_w, audio_gate_w, levels, video_pos, audio_pos,
):
    width = HEADS * HD
    rank = lax.axis_index(AXES)
    frame = rank // (NX * NY * NZ * NC // video_pos.shape[0])
    frequency = 10000.0 ** (-(INDEX * np.float32(2.0)) / WIDTH_OF)
    table = jnp.asarray(
        np.concatenate(
            [
                np.stack([frequency, SIGN, SECTION]),
                np.zeros((5, HD)),
                np.arange(HD)[:, None] == PARTNER[None, :],
            ]
        ).astype(np.float32)
    )
    heads = (video_q, video_k, video_v, audio_q, audio_k, audio_v)
    packed = pl.pallas_call(
        prep_kernel,
        out_shape=jax.ShapeDtypeStruct((NZ, 3, HPG, T_L, HD), jnp.bfloat16),
        in_specs=[ANY] * 9,
        out_specs=VMEM,
        scratch_shapes=[
            pltpu.SMEM(video_pos.shape, jnp.int32),
            pltpu.SMEM(audio_pos.shape, jnp.int32),
            *(pltpu.VMEM(array.shape, jnp.bfloat16) for array in heads),
            pltpu.VMEM(table.shape, jnp.float32),
            pltpu.SemaphoreType.DMA((9,)),
        ],
        compiler_params=params(60),
    )(video_pos, audio_pos, *heads, table)
    got = lax.all_to_all(packed, ("zl", "zh"), split_axis=0, concat_axis=0, tiled=True)
    q_mine, kv_mine = pl.pallas_call(
        arrange_kernel,
        out_shape=(
            jax.ShapeDtypeStruct((HPG, ROWS, HD), jnp.bfloat16),
            jax.ShapeDtypeStruct((2, HPG, ROWS, HD), jnp.bfloat16),
        ),
        in_specs=[VMEM],
        out_specs=(VMEM, VMEM),
        compiler_params=params(32),
    )(got)

    video_gate = frame_gate(levels, frame, video_gate_w)
    audio_gate = frame_gate(levels, frame, audio_gate_w)
    kv_left = shift(kv_mine, "x", 1, NX)
    kv_right = shift(kv_mine, "x", NX - 1, NX)
    steps = (1, NY - 1, 2)
    q_far = [shift(q_mine, "y", step, NY) for step in steps]
    kv_left, kv_right, kv_held, q_far[0], q_far[1], video_gate, audio_gate = (
        lax.optimization_barrier(
            (kv_left, kv_right, kv_mine, q_far[0], q_far[1], video_gate, audio_gate)
        )
    )
    k_far = shift(kv_left[0], "x", 1, NX)
    v_far = shift(kv_right[1], "x", NX - 1, NX)
    k_far, v_far, q_far[2] = lax.optimization_barrier((k_far, v_far, q_far[2]))
    pairs = [kv_held, kv_left, kv_right]
    pairs = pairs + [shift(kv, "c", 1, NC) for kv in pairs]
    splits = [k_far, v_far, shift(k_far, "c", 1, NC), shift(v_far, "c", 1, NC)]

    partial, keys, values = attention(q_far[0], pairs, splits, None)
    video_w, audio_w = video_out_w, audio_out_w
    back = [shift(partial, "y", NY - steps[0], NY)]
    wv_other = shift(video_w, "c", 1, NC)
    wa_other = shift(audio_w, "c", 1, NC)
    queries, partial = lax.optimization_barrier((q_far[1], partial))
    partial = attention(queries, (), (), (keys, values))
    back.append(shift(partial, "y", NY - steps[1], NY))
    queries, partial, back[0] = lax.optimization_barrier((q_far[2], partial, back[0]))
    partial = attention(queries, (), (), (keys, values))
    back.append(shift(partial, "y", NY - steps[2], NY))
    queries, partial, back[1] = lax.optimization_barrier((q_mine, partial, back[1]))
    back = [attention(queries, (), (), (keys, values))] + back
    zl = lax.axis_index("zl")
    c = lax.axis_index("c")
    a_shape = jax.ShapeDtypeStruct((HALF, HPG * HD), jnp.bfloat16)
    keep, send = pl.pallas_call(
        merge_kernel,
        out_shape=(a_shape, a_shape),
        in_specs=[SMEM] + [VMEM] * NY,
        out_specs=(VMEM, VMEM),
        scratch_shapes=[pltpu.VMEM((ROWS, HPG * HD), jnp.bfloat16)],
        compiler_params=params(32),
    )(jnp.full((1,), zl, jnp.int32), *back)
    came = shift(send, "zl", 1, NZL)
    same = jnp.full((1,), zl == c, jnp.int32)
    weights = (video_out_w, wv_other, audio_out_w, wa_other)
    cols = 768
    half = width // 2
    scratch = [
        pltpu.VMEM((2, width // cols, HPG * HD, cols), jnp.bfloat16),
        pltpu.SemaphoreType.DMA((2, width // cols)),
    ]
    part = pl.pallas_call(
        project_kept_kernel,
        out_shape=jax.ShapeDtypeStruct((HALF, width), jnp.float32),
        in_specs=[SMEM, VMEM] + [HBM] * 4,
        out_specs=VMEM,
        scratch_shapes=scratch,
        compiler_params=params(20),
        cost_estimate=pl.CostEstimate(
            flops=8 * HALF * HPG * HD * width, bytes_accessed=6 << 20, transcendentals=0
        ),
    )(same, keep, *weights)
    side = jax.ShapeDtypeStruct((T_L, half), jnp.bfloat16)
    own, right_a, right_b, far_a, far_b, left_a, left_b = pl.pallas_call(
        project_came_kernel,
        out_shape=(jax.ShapeDtypeStruct((T_L, width), jnp.bfloat16),) + (side,) * 6,
        in_specs=[SMEM, VMEM, VMEM] + [HBM] * 4,
        out_specs=(VMEM,) * 7,
        scratch_shapes=scratch,
        compiler_params=params(20),
    )(same, came, part, *weights)
    far_a = shift(far_a, "zh", 1, NZH)
    far_b = shift(far_b, "zh", NZH - 1, NZH)
    b_one = shift(right_b, "zh", 1, NZH)
    a_two = shift(left_a, "zh", NZH - 1, NZH)

    def add(one, two):
        return (one.astype(jnp.float32) + two.astype(jnp.float32)).astype(jnp.bfloat16)

    a_one = shift(add(right_a, far_a), "zh", 1, NZH)
    b_two = shift(add(left_b, far_b), "zh", NZH - 1, NZH)
    return tuple(
        pl.pallas_call(
            finish_kernel,
            out_shape=(
                jax.ShapeDtypeStruct(video_x.shape, jnp.bfloat16),
                jax.ShapeDtypeStruct(audio_x.shape, jnp.bfloat16),
            ),
            in_specs=[VMEM] * 9,
            out_specs=(VMEM, VMEM),
            compiler_params=params(32),
        )(own, a_one, a_two, b_one, b_two, video_x, audio_x, video_gate, audio_gate)
    )


def solution(mesh):
    fine = Mesh(mesh.devices.reshape(NX, NY, NZL, NZH, NC), AXES)
    tokens3 = P(AXES, None, None)
    tokens2 = P(AXES, None)
    weights = P(("zh", "c"), None)
    return jax.shard_map(
        local,
        mesh=fine,
        in_specs=(
            tokens3, tokens3, tokens3, tokens3, tokens3, tokens3,
            tokens2, tokens2, weights, weights, P(), P(), P(), P(), P(AXES),
        ),
        out_specs=(tokens2, tokens2),
        check_vma=False,
    )
```
